256 devices in a mesh: ctx: 16 (over y_lo, z), chan: 16 (over x, y_hi, core).
Axes of the slice: x: 4, y: 4 (y_hi: 2, y_lo: 2; y = y_hi * 2 + y_lo), z: 8, core: 2. Of those that a mesh axis runs over, the one named last changes fastest.
Arguments:
- query_rows: bfloat16 [4096, 4096], P('ctx', 'chan'), may hold values from -6 to 6
- key_rows: bfloat16 [4096, 4096], P('ctx', 'chan'), may hold values from -6 to 6
- value_rows: bfloat16 [4096, 4096], P('ctx', 'chan'), may hold values from -6 to 6
- residues: float32 [16, 4096], P(None, 'chan'), may hold values from -4 to 4
- decays: float32 [16, 4096], P(None, 'chan'), may hold values from 0.5 to 117
- skip_gain: float32 [4096], P('chan'), may hold values from -4 to 4
- out_weight: bfloat16 [4096, 8192], P('chan'), may hold values from -0.125 to 0.125
- cotangent: bfloat16 [4096, 8192], P('ctx', 'chan'), may hold values from -6 to 6
Outputs:
- layer_out: bfloat16 [4096, 8192], P('ctx', 'chan')
- query_grad: bfloat16 [4096, 4096], P('ctx', 'chan')
- key_grad: bfloat16 [4096, 4096], P('ctx', 'chan')
- value_grad: bfloat16 [4096, 4096], P('ctx', 'chan')
- residue_grad: float32 [16, 4096], P(None, 'chan')
- skip_grad: float32 [4096], P('chan')
- weight_grad: float32 [4096, 8192], P('chan', 'ctx')
The draws below stay inside these ranges and needn't reach their ends.
All inputs are finite; a program needn't handle non-finite values.
Results may differ from the reference program's by a relative error of at most 0.024.
Values may be sent and summed in bfloat16 or wider, within the bound.
No kernel may reach another device: no remote copies, remote signals or barrier semaphores. Data moves between devices by JAX's collectives and lax.ppermute only.
A program may use at most 128 MiB of HBM per device.

```python
import math
import jax
import jax.numpy as jnp
from jax import lax

D = 8192
C = 4096
MODES = 16
TOK_DEV = 256
LENGTH = 4096
N_CTX = 16
N_CHAN = 16


def spiked(array, stream_key, source, target, parts, factor):
    def block_of(dim):
        return (jnp.arange(array.shape[dim]) // (array.shape[dim] // parts)).reshape((-1,) + (1,) * (array.ndim - 1 - dim))

    one_side = jax.random.permutation(stream_key, parts)[block_of(target)]
    far = (block_of(target) + parts // 2) % parts
    return jnp.where((block_of(source) == one_side) | (block_of(source) == far), factor * array, array)


def shard_levels(key, dims, shards, least, largest):
    gain = 1.0
    for position, blocks in shards:
        draws = jax.random.uniform(jax.random.fold_in(jax.random.fold_in(key, 6), position), (blocks,), jnp.float32, least / len(shards), largest / len(shards))
        gain = gain * jnp.repeat(jnp.exp(draws), dims[position] // blocks).reshape((-1,) + (1,) * (len(dims) - 1 - position))
    return gain


def centred(key, dims, width, reach, split=(), kind=jnp.bfloat16):
    drawn = width * jax.random.normal(key, dims, jnp.float32)
    if split:
        drawn = drawn * shard_levels(key, dims, split, -0.22, 0.18)
    return jnp.clip(drawn, -reach, reach).astype(kind)


def bell_draw_with(key, extent, scale, reach, cuts, heavy, kind=jnp.bfloat16):
    entries = scale * jax.random.normal(key, extent, jnp.float32)
    if cuts:
        entries = entries * shard_levels(key, extent, cuts, -0.22, 0.18)
    return jnp.clip(spiked(entries, jax.random.fold_in(key, 3), *heavy), -reach, reach).astype(kind)


def setup_inputs(seed: int = 0) -> dict:
    splits = jax.random.split(jax.random.key(seed), 9)
    return {
        "query_rows": centred(splits[0], (LENGTH, C), 1.0, 6.0, ((0, 16), (1, 16))),
        "key_rows": centred(splits[1], (LENGTH, C), 1.0, 6.0, ((0, 16), (1, 16))),
        "value_rows": centred(splits[2], (LENGTH, C), 1.0, 6.0, ((0, 16), (1, 16))),
        "residues": centred(splits[3], (MODES, C), 1.0, 4.0, ((1, 16),), jnp.float32),
        "decays": jnp.clip(jnp.exp(math.log(117.0) - 5.4553211 * jax.random.uniform(splits[4], (MODES, C), jnp.float32) ** shard_levels(splits[4], (MODES, C), ((1, 16),), -0.2, 0.2)), 0.5, 117.0),
        "skip_gain": centred(splits[5], (C,), 1.0, 4.0, ((0, 16),), jnp.float32),
        "out_weight": bell_draw_with(splits[6], (C, D), C ** -0.5, 0.125, ((0, 16),), (0, 1, 16, 2.0)),
        "cotangent": bell_draw_with(splits[7], (LENGTH, D), 1.0, 6.0, ((0, 16), (1, 16)), (0, 1, 16, 2.0)),
    }


def mode_terms(decays):
    mode_rates = decays / LENGTH
    mode_gains = jnp.sqrt(-jnp.expm1(-2.0 * mode_rates) / MODES)
    return (mode_rates, mode_gains)

def position_offsets():
    return jnp.arange(LENGTH, dtype=jnp.int32).astype(jnp.float32)

def build_impulse(residues, mode_rates, mode_gains):
    offsets = position_offsets()

    def add_mode(running, mode_index):
        decay_curve = jnp.exp(-offsets[:, None] * mode_rates[mode_index][None, :])
        return (running + (residues[mode_index] * mode_gains[mode_index])[None, :] * decay_curve, None)
    impulse, _ = lax.scan(add_mode, jnp.zeros((LENGTH, C), jnp.float32), jnp.arange(MODES, dtype=jnp.int32))
    return impulse

def spectral(signal_rows, kernel_rows, conjugate):
    first_spec = jnp.fft.rfft(signal_rows, n=2 * LENGTH, axis=0)
    second_spec = jnp.fft.rfft(kernel_rows, n=2 * LENGTH, axis=0)
    if conjugate:
        second_spec = jnp.conj(second_spec)
    return jnp.fft.irfft(first_spec * second_spec, n=2 * LENGTH, axis=0)[:LENGTH]

def chan_blocks(gated_rows, out_weight):
    block_width = C // N_CHAN

    def add_block(running, block_index):
        first_index = block_index * block_width
        left_rows = lax.dynamic_slice_in_dim(gated_rows, first_index, block_width, 1)
        right_rows = lax.dynamic_slice_in_dim(out_weight, first_index, block_width, 0)
        part_sum = jnp.dot(left_rows, right_rows, preferred_element_type=jnp.float32).astype(jnp.bfloat16)
        part_sum = lax.optimization_barrier(part_sum)
        return (running + part_sum.astype(jnp.float32), None)
    totals, _ = lax.scan(add_block, jnp.zeros((LENGTH, D), jnp.float32), jnp.arange(N_CHAN, dtype=jnp.int32))
    return totals.astype(jnp.bfloat16)

def ctx_blocks(gated_rows, cotangent):

    def add_block(running, block_index):
        first_index = block_index * TOK_DEV
        left_rows = lax.dynamic_slice_in_dim(gated_rows, first_index, TOK_DEV, 0)
        right_rows = lax.dynamic_slice_in_dim(cotangent, first_index, TOK_DEV, 0)
        part_sum = jnp.dot(left_rows.T, right_rows, preferred_element_type=jnp.float32).astype(jnp.bfloat16)
        part_sum = lax.optimization_barrier(part_sum)
        return (running + part_sum.astype(jnp.float32), None)
    totals, _ = lax.scan(add_block, jnp.zeros((C, D), jnp.float32), jnp.arange(N_CTX, dtype=jnp.int32))
    return totals

def reference(query_rows, key_rows, value_rows, residues, decays, skip_gain, out_weight, cotangent):
    product = key_rows.astype(jnp.float32) * value_rows.astype(jnp.float32)
    mode_rates, mode_gains = mode_terms(decays)
    impulse = build_impulse(residues, mode_rates, mode_gains)
    convolved = spectral(product, impulse, False)
    mixed_sum = convolved + skip_gain[None, :] * product
    queries = query_rows.astype(jnp.float32)
    gated_rows = (queries * mixed_sum).astype(jnp.bfloat16)
    layer_out = chan_blocks(gated_rows, out_weight)
    upstream = jnp.dot(cotangent, out_weight.T, preferred_element_type=jnp.float32)
    query_grad = (upstream * mixed_sum).astype(jnp.bfloat16)
    drive_rows = upstream * queries
    backward_conv = spectral(drive_rows, impulse, True)
    product_grad = backward_conv + skip_gain[None, :] * drive_rows
    key_grad = (product_grad * value_rows.astype(jnp.float32)).astype(jnp.bfloat16)
    value_grad = (product_grad * key_rows.astype(jnp.float32)).astype(jnp.bfloat16)
    lag_sum = spectral(drive_rows, product, True)
    offsets = position_offsets()

    def mode_total(mode_index):
        decay_curve = jnp.exp(-offsets[:, None] * mode_rates[mode_index][None, :])
        return mode_gains[mode_index] * lax.optimization_barrier(jnp.sum(lag_sum * decay_curve, axis=0))
    residue_grad = lax.map(mode_total, jnp.arange(MODES, dtype=jnp.int32))
    skip_grad = lax.optimization_barrier(jnp.sum(drive_rows * product, axis=0))
    weight_grad = ctx_blocks(gated_rows, cotangent)
    return (layer_out, query_grad, key_grad, value_grad, residue_grad, skip_grad, weight_grad)
```

```python
import jax
import jax.numpy as jnp
from jax import lax
from jax.experimental import pallas as pl
from jax.experimental.pallas import tpu as pltpu
from jax.sharding import PartitionSpec as P

F32 = jnp.float32
BF16 = jnp.bfloat16
LANES = 128
SUB = 16
HALF = 8
CHIP_MASKS = tuple(range(0, 16, 2))


def traded(value, axis, mask):
    pairs = [(source, source ^ mask) for source in range(lax.axis_size(axis))]
    return lax.ppermute(value, axis, pairs)


def strided(ref, offset, half):
    return ref[pl.ds(offset + half * HALF * SUB, HALF, stride=SUB), :]


def forward_local(key_ref, value_ref, rate_ref, weight_ref, skip_ref, state_ref, mixed_ref, product, carried, scaled):
    product[...] = key_ref[...].astype(F32) * value_ref[...].astype(F32)
    rates = rate_ref[...]
    weights = weight_ref[...]
    pole = jnp.exp(-rates)
    leap = jnp.exp(-float(SUB) * rates)
    state = jnp.zeros_like(rates)
    for block in range(SUB):
        carried[pl.ds(block * SUB, SUB), :] = state
        inner = jnp.broadcast_to(product[pl.ds(block * SUB, 1), :], rates.shape)
        for step in range(1, SUB):
            inner = pole * inner + product[pl.ds(block * SUB + step, 1), :]
        state = leap * state + inner
    state_ref[...] = state
    taps = []
    power = weights
    for step in range(SUB):
        taps.append(jnp.sum(power, axis=0, keepdims=True))
        power = power * pole
        scaled[pl.ds(step * SUB, SUB), :] = power
    taps[0] = taps[0] + skip_ref[...]
    for half in range(2):
        held = [strided(carried, mode, half) for mode in range(SUB)]
        signal = [strided(product, step, half) for step in range(SUB)]
        for step in range(SUB):
            total = taps[0] * signal[step]
            for lag in range(1, step + 1):
                total = total + taps[lag] * signal[step - lag]
            for mode in range(SUB):
                total = total + scaled[pl.ds(step * SUB + mode, 1), :] * held[mode]
            mixed_ref[pl.ds(step + half * HALF * SUB, HALF, stride=SUB), :] = total


def block_decay(rates, mode, half, backward):
    place = lax.broadcasted_iota(jnp.int32, (HALF, LANES), 0).astype(F32) + float(half * HALF)
    distance = float(SUB - 1) - place if backward else place
    return jnp.exp(-float(SUB) * distance * rates[mode : mode + 1, :])


def forward_mix(position_ref, local_ref, query_ref, rate_ref, weight_ref, state_ref, out_weight_ref, *rest):
    mixed_ref, gated_ref = rest[:2]
    other_refs = rest[2:10]
    mine_refs = rest[10:18]
    scaled, narrow = rest[18:]
    for tile in range(2):
        lanes = pl.ds(tile * LANES, LANES)
        narrow[...] = local_ref[:, lanes]
        rates = rate_ref[:, lanes]
        weights = weight_ref[:, lanes]
        entering = state_ref[:, lanes]
        pole = jnp.exp(-rates)
        power = weights
        for step in range(SUB):
            power = power * pole
            scaled[pl.ds(step * SUB, SUB), :] = power
        for half in range(2):
            held = [
                block_decay(rates, mode, half, False) * entering[mode : mode + 1, :]
                for mode in range(SUB)
            ]
            for step in range(SUB):
                rows = pl.ds(step + half * HALF * SUB, HALF, stride=SUB)
                total = narrow[rows, :]
                for mode in range(SUB):
                    total = total + scaled[pl.ds(step * SUB + mode, 1), :] * held[mode]
                narrow[rows, :] = total
        mixed_ref[:, lanes] = narrow[...]
    gated = query_ref[...].astype(F32) * mixed_ref[...]
    rounded = gated.astype(BF16)
    gated_ref[...] = gated.T.astype(BF16)
    place = position_ref[0]
    for index, mask in enumerate(CHIP_MASKS):
        for refs, flip in ((other_refs, 1), (mine_refs, 0)):
            first = pl.multiple_of((place ^ (mask | flip)) * 512, 512)
            refs[index][...] = jnp.dot(
                rounded, out_weight_ref[:, pl.ds(first, 512)], preferred_element_type=F32
            ).astype(BF16)


def upstream_rows(position_ref, query_ref, mixed_ref, out_weight_ref, *rest):
    arrived = rest[:16]
    query_grad_ref, drive_ref = rest[16:]
    place = position_ref[0]
    total = jnp.zeros(query_ref.shape, F32)
    for mask in range(16):
        first = pl.multiple_of((place ^ mask) * 512, 512)
        total = total + lax.dot_general(
            arrived[mask][...],
            out_weight_ref[:, pl.ds(first, 512)],
            (((1,), (1,)), ((), ())),
            preferred_element_type=F32,
        )
    query_grad_ref[...] = (total * mixed_ref[...]).astype(BF16)
    drive_ref[...] = total * query_ref[...].astype(F32)


def backward_local(drive_ref, key_ref, value_ref, rate_ref, weight_ref, skip_ref, state_ref, local_ref, sums_ref, product, carried):
    product[...] = key_ref[...].astype(F32) * value_ref[...].astype(F32)
    rates = rate_ref[...]
    weights = weight_ref[...]
    pole = jnp.exp(-rates)
    leap = jnp.exp(-float(SUB) * rates)
    state = jnp.zeros_like(rates)
    for block in reversed(range(SUB)):
        carried[pl.ds(block * SUB, SUB), :] = state
        inner = jnp.broadcast_to(drive_ref[pl.ds(block * SUB + SUB - 1, 1), :], rates.shape)
        for step in reversed(range(SUB - 1)):
            inner = pole * inner + drive_ref[pl.ds(block * SUB + step, 1), :]
        state = leap * state + inner
    state_ref[...] = state
    sums_ref[...] = jnp.zeros(sums_ref.shape, F32)
    for half in range(2):
        drives = [strided(drive_ref, step, half) for step in range(SUB)]
        signal = [strided(product, step, half) for step in range(SUB)]
        totals = [skip_ref[...] * drive for drive in drives]
        direct = drives[0] * signal[0]
        for step in range(1, SUB):
            direct = direct + drives[step] * signal[step]
        sums_ref[pl.ds(SUB, 1), :] += jnp.sum(direct, axis=0, keepdims=True)
        for mode in range(SUB):
            running = strided(carried, mode, half)
            gathered = jnp.zeros_like(running)
            for step in reversed(range(SUB)):
                running = pole[mode : mode + 1, :] * running + drives[step]
                totals[step] = totals[step] + weights[mode : mode + 1, :] * running
                gathered = gathered + signal[step] * running
            sums_ref[pl.ds(mode, 1), :] += jnp.sum(gathered, axis=0, keepdims=True)
        for step in range(SUB):
            local_ref[pl.ds(step + half * HALF * SUB, HALF, stride=SUB), :] = totals[step]


def backward_mix(local_ref, key_ref, value_ref, rate_ref, weight_ref, gain_ref, later_ref, state_ref, sums_ref, key_grad_ref, value_grad_ref, part_ref, scaled, grads):
    rates = rate_ref[...]
    later = later_ref[...]
    pole = jnp.exp(-rates)
    power = weight_ref[...]
    for step in reversed(range(SUB)):
        power = power * pole
        scaled[pl.ds(step * SUB, SUB), :] = power
    for half in range(2):
        held = [
            block_decay(rates, mode, half, True) * later[mode : mode + 1, :] for mode in range(SUB)
        ]
        for step in range(SUB):
            total = strided(local_ref, step, half)
            for mode in range(SUB):
                total = total + scaled[pl.ds(step * SUB + mode, 1), :] * held[mode]
            grads[pl.ds(step + half * HALF * SUB, HALF, stride=SUB), :] = total
    product_grad = grads[...]
    key_grad_ref[...] = (product_grad * value_ref[...].astype(F32)).astype(BF16)
    value_grad_ref[...] = (product_grad * key_ref[...].astype(F32)).astype(BF16)
    part_ref[pl.ds(0, SUB), :] = gain_ref[...] * (
        sums_ref[pl.ds(0, SUB), :] + pole * state_ref[...] * later
    )
    part_ref[pl.ds(SUB, HALF), :] = sums_ref[pl.ds(SUB, HALF), :]


def weight_rows(position_ref, *rest):
    gated = rest[:16]
    arrived = rest[16:32]
    out_ref = rest[32]
    held, semaphores = rest[33:]
    copies = [
        pltpu.make_async_copy(arrived[index], held.at[index], semaphores.at[index])
        for index in range(16)
    ]
    for copy in copies:
        copy.start()
    for copy in copies:
        copy.wait()
    turn = position_ref[0] ^ position_ref[1]
    total = jnp.zeros(out_ref.shape, F32)
    for mask in range(16):
        total = total + jnp.dot(
            gated[mask][...], held[turn ^ mask], preferred_element_type=F32
        )
    out_ref[...] = total


VMEM = pl.BlockSpec(memory_space=pltpu.VMEM)
SMEM = pl.BlockSpec(memory_space=pltpu.SMEM)
ANY = pl.BlockSpec(memory_space=pl.ANY)
LIMIT = pltpu.CompilerParams(vmem_limit_bytes=40 * 1024 * 1024)


def tile_of(rows):
    return pl.BlockSpec((rows, LANES), lambda tile: (0, tile))


def shape_of(rows, columns, kind=F32):
    return jax.ShapeDtypeStruct((rows, columns), kind)


def decayed(rates, distance, present):
    reach = jnp.maximum(distance, 0).astype(F32)
    return jnp.where(present, jnp.exp(-reach * rates), 0.0)


def chained(state, rates, rank, tokens, backward):
    low = rank & 3
    high = rank >> 2
    near = [(low ^ mask, traded(state, "ctx", mask) if mask else state) for mask in range(4)]
    inside = 0.0
    whole = 0.0
    for spot, value in near:
        if backward:
            inside = inside + decayed(rates, tokens * (spot - low - 1), spot > low) * value
            whole = whole + decayed(rates, tokens * spot, True) * value
        else:
            inside = inside + decayed(rates, tokens * (low - 1 - spot), spot < low) * value
            whole = whole + decayed(rates, tokens * (3 - spot), True) * value
    across = 0.0
    for mask in range(1, 4):
        spot = high ^ mask
        value = traded(whole, "ctx", 4 * mask)
        if backward:
            across = across + decayed(rates, 4 * tokens * (spot - high - 1), spot > high) * value
        else:
            across = across + decayed(rates, 4 * tokens * (high - 1 - spot), spot < high) * value
    span = 3 - low if backward else low
    return inside + decayed(rates, tokens * span, True) * across


def summed(part):
    for scale in (1, 4):
        first, second, third = (traded(part, "ctx", scale * mask) for mask in (1, 2, 3))
        part = (part + first) + (second + third)
    return part


def spread(block):
    blocks = {}
    for mask in CHIP_MASKS:
        blocks[mask] = traded(block, "chan", mask) if mask else block
    for mask in CHIP_MASKS:
        blocks[mask | 1] = traded(blocks[mask], "chan", 1)
    return [blocks[mask] for mask in range(16)]


def on_device(query_rows, key_rows, value_rows, residues, decays, skip_gain, out_weight, cotangent):
    tokens, width = query_rows.shape
    modes = residues.shape[0]
    ctx_count = lax.axis_size("ctx")
    chan_count = lax.axis_size("chan")
    rank = lax.axis_index("ctx")
    place = lax.axis_index("chan")
    positions = jnp.stack([place, rank]).astype(jnp.int32)
    rates = decays / (tokens * ctx_count)
    gains = jnp.sqrt(-jnp.expm1(-2.0 * rates) / modes)
    weights = residues * gains
    skip_row = skip_gain.reshape(1, width)
    tiles = width // LANES
    rows = tile_of(tokens)
    few = tile_of(modes)
    one = tile_of(1)
    sums = tile_of(modes + HALF)
    block_scratch = pltpu.VMEM((tokens, LANES), F32)

    columns = spread(cotangent)
    turned = lax.ppermute(
        cotangent,
        ("ctx", "chan"),
        [
            (first * chan_count + second, second * chan_count + first)
            for first in range(ctx_count)
            for second in range(chan_count)
        ],
    )

    state, local = pl.pallas_call(
        forward_local,
        grid=(tiles,),
        in_specs=[rows, rows, few, few, one],
        out_specs=[few, rows],
        out_shape=[shape_of(modes, width), shape_of(tokens, width)],
        scratch_shapes=[block_scratch] * 3,
        name="forward_local",
    )(key_rows, value_rows, rates, weights, skip_row)
    entering = chained(state, rates, rank, tokens, False)
    block_width = cotangent.shape[1]
    mixed, gated, *parts = pl.pallas_call(
        forward_mix,
        in_specs=[SMEM] + [VMEM] * 6,
        out_specs=[VMEM] * 18,
        out_shape=[shape_of(tokens, width), shape_of(width, tokens, BF16)]
        + [shape_of(tokens, block_width, BF16)] * 16,
        scratch_shapes=[block_scratch] * 2,
        compiler_params=LIMIT,
        name="forward_mix",
    )(positions, local, query_rows, rates, weights, entering, out_weight)

    gated_blocks = [traded(gated, "ctx", mask) if mask else gated for mask in range(ctx_count)]

    layer_total = 0.0
    for index, mask in enumerate(CHIP_MASKS):
        met = parts[8 + index].astype(F32) + traded(parts[index], "chan", 1).astype(F32)
        met = met.astype(BF16)
        arrived = traded(met, "chan", mask) if mask else met
        layer_total = layer_total + arrived.astype(F32)
    layer_out = layer_total.astype(BF16)

    query_grad, drive = pl.pallas_call(
        upstream_rows,
        in_specs=[SMEM] + [VMEM] * 19,
        out_specs=[VMEM] * 2,
        out_shape=[shape_of(tokens, width, BF16), shape_of(tokens, width)],
        compiler_params=LIMIT,
        name="upstream_rows",
    )(positions, query_rows, mixed, out_weight, *columns)
    last_state, back_local, sum_part = pl.pallas_call(
        backward_local,
        grid=(tiles,),
        in_specs=[rows, rows, rows, few, few, one],
        out_specs=[few, rows, sums],
        out_shape=[shape_of(modes, width), shape_of(tokens, width), shape_of(modes + HALF, width)],
        scratch_shapes=[block_scratch] * 2,
        name="backward_local",
    )(drive, key_rows, value_rows, rates, weights, skip_row)
    later = chained(last_state, rates, rank, tokens, True)
    key_grad, value_grad, part = pl.pallas_call(
        backward_mix,
        grid=(tiles,),
        in_specs=[rows, rows, rows, few, few, few, few, few, sums],
        out_specs=[rows, rows, sums],
        out_shape=[
            shape_of(tokens, width, BF16),
            shape_of(tokens, width, BF16),
            shape_of(modes + HALF, width),
        ],
        scratch_shapes=[block_scratch] * 2,
        name="backward_mix",
    )(back_local, key_rows, value_rows, rates, weights, gains, later, state, sum_part)
    part = summed(part)

    turned_blocks = spread(turned)
    weight_grad = pl.pallas_call(
        weight_rows,
        in_specs=[SMEM] + [VMEM] * 16 + [ANY] * 16,
        out_specs=VMEM,
        out_shape=shape_of(width, block_width),
        scratch_shapes=[
            pltpu.VMEM((chan_count, tokens, block_width), BF16),
            pltpu.SemaphoreType.DMA((chan_count,)),
        ],
        compiler_params=LIMIT,
        name="weight_rows",
    )(positions, *gated_blocks, *turned_blocks)
    return (
        layer_out,
        query_grad,
        key_grad,
        value_grad,
        part[:modes],
        part[modes],
        weight_grad,
    )


def solution(mesh):
    placed = (
        P("ctx", "chan"),
        P("ctx", "chan"),
        P("ctx", "chan"),
        P(None, "chan"),
        P(None, "chan"),
        P("chan"),
        P("chan", None),
        P("ctx", "chan"),
    )
    return jax.shard_map(
        on_device,
        mesh=mesh,
        in_specs=placed,
        out_specs=(
            P("ctx", "chan"),
            P("ctx", "chan"),
            P("ctx", "chan"),
            P("ctx", "chan"),
            P(None, "chan"),
            P("chan"),
            P("chan", "ctx"),
        ),
        check_vma=False,
    )
```

```python
import functools

import jax
import jax.numpy as jnp
from jax import lax
from jax.experimental import pallas as pl
from jax.experimental.pallas import tpu as pltpu
from jax.sharding import PartitionSpec as P

F32 = jnp.float32
BF16 = jnp.bfloat16
LANES = 128
SUB = 16
HALF = 8
CHIP_MASKS = tuple(range(0, 16, 2))


def traded(value, axis, mask):
    pairs = [(source, source ^ mask) for source in range(lax.axis_size(axis))]
    return lax.ppermute(value, axis, pairs)


def strided(ref, offset, half):
    return ref[pl.ds(offset + half * HALF * SUB, HALF, stride=SUB), :]


def forward_local(key_ref, value_ref, rate_ref, weight_ref, skip_ref, state_ref, mixed_ref, product, carried, scaled):
    product[...] = key_ref[...].astype(F32) * value_ref[...].astype(F32)
    rates = rate_ref[...]
    weights = weight_ref[...]
    pole = jnp.exp(-rates)
    leap = jnp.exp(-float(SUB) * rates)
    state = jnp.zeros_like(rates)
    for block in range(SUB):
        carried[pl.ds(block * SUB, SUB), :] = state
        inner = jnp.broadcast_to(product[pl.ds(block * SUB, 1), :], rates.shape)
        for step in range(1, SUB):
            inner = pole * inner + product[pl.ds(block * SUB + step, 1), :]
        state = leap * state + inner
    state_ref[...] = state
    taps = []
    power = weights
    for step in range(SUB):
        taps.append(jnp.sum(power, axis=0, keepdims=True))
        power = power * pole
        scaled[pl.ds(step * SUB, SUB), :] = power
    taps[0] = taps[0] + skip_ref[...]
    for half in range(2):
        held = [strided(carried, mode, half) for mode in range(SUB)]
        signal = [strided(product, step, half) for step in range(SUB)]
        for step in range(SUB):
            total = taps[0] * signal[step]
            for lag in range(1, step + 1):
                total = total + taps[lag] * signal[step - lag]
            for mode in range(SUB):
                total = total + scaled[pl.ds(step * SUB + mode, 1), :] * held[mode]
            mixed_ref[pl.ds(step + half * HALF * SUB, HALF, stride=SUB), :] = total


def block_decay(rates, mode, half, backward):
    place = lax.broadcasted_iota(jnp.int32, (HALF, LANES), 0).astype(F32) + float(half * HALF)
    distance = float(SUB - 1) - place if backward else place
    return jnp.exp(-float(SUB) * distance * rates[mode : mode + 1, :])


def falling(rates, distance):
    reach = jnp.maximum(distance, 0).astype(F32)
    present = jnp.where(distance >= 0, 1.0, 0.0).astype(F32)
    return jnp.exp(-reach * rates) * present


def near_sums(backward, tokens, position_ref, rate_ref, value_refs, inside_ref, whole_ref):
    values = [ref[...] for ref in value_refs]
    rates = rate_ref[...]
    modes = rates.shape[0]
    low = position_ref[1] & 3
    inside = jnp.zeros_like(rates)
    whole = jnp.zeros_like(rates)
    for mask in range(4):
        spot = low ^ mask
        state = values[mask][:modes]
        gap = spot - low - 1 if backward else low - 1 - spot
        far = spot if backward else 3 - spot
        inside = inside + falling(rates, tokens * gap) * state
        whole = whole + falling(rates, tokens * far) * state
    inside_ref[...] = inside
    whole_ref[pl.ds(0, modes), :] = whole
    if values[0].shape[0] > modes:
        sums = [value[modes:] for value in values]
        whole_ref[pl.ds(modes, sums[0].shape[0]), :] = (sums[0] + sums[1]) + (sums[2] + sums[3])


def forward_near(tokens, position_ref, rate_ref, *rest):
    own_ref, arrived_ref, inside_ref, whole_ref, pair_ref = rest[4:]
    near_sums(False, tokens, position_ref, rate_ref, rest[:4], inside_ref, whole_ref)
    pair_ref[0] = own_ref[...]
    pair_ref[1] = arrived_ref[...]


def open_far(first_ref, third_ref, even_ref, odd_ref):
    even_ref[...] = first_ref[0]
    odd_ref[...] = third_ref[1]


def stack_blocks(refs, out_ref):
    pair, first, third, even, odd = refs
    for index, block in enumerate((pair.at[0], pair.at[1], first.at[0], first.at[1])):
        out_ref[index] = block[...]
    for index, block in enumerate((even, odd, third.at[0], third.at[1])):
        out_ref[4 + index] = block[...]


def joined(backward, tokens, position_ref, rates, inside, across):
    low = position_ref[1] & 3
    high = lax.shift_right_logical(position_ref[1], 2)
    total = jnp.zeros_like(rates)
    for mask in range(1, 4):
        spot = high ^ mask
        gap = spot - high - 1 if backward else high - 1 - spot
        total = total + falling(rates, 4 * tokens * gap) * across[mask - 1]
    span = 3 - low if backward else low
    return inside + falling(rates, tokens * span) * total


def forward_mix(position_ref, local_ref, query_ref, rate_ref, weight_ref, inside_ref, first_ref, second_ref, third_ref, mixed_ref, gated_ref, turned_ref, entering_ref, scaled, narrow):
    tokens = local_ref.shape[0]
    for tile in range(2):
        lanes = pl.ds(tile * LANES, LANES)
        narrow[...] = local_ref[:, lanes]
        rates = rate_ref[:, lanes]
        weights = weight_ref[:, lanes]
        across = [ref[:, lanes] for ref in (first_ref, second_ref, third_ref)]
        entering = joined(False, tokens, position_ref, rates, inside_ref[:, lanes], across)
        entering_ref[:, lanes] = entering
        pole = jnp.exp(-rates)
        power = weights
        for step in range(SUB):
            power = power * pole
            scaled[pl.ds(step * SUB, SUB), :] = power
        for half in range(2):
            held = [
                block_decay(rates, mode, half, False) * entering[mode : mode + 1, :]
                for mode in range(SUB)
            ]
            for step in range(SUB):
                rows = pl.ds(step + half * HALF * SUB, HALF, stride=SUB)
                total = narrow[rows, :]
                for mode in range(SUB):
                    total = total + scaled[pl.ds(step * SUB + mode, 1), :] * held[mode]
                narrow[rows, :] = total
        mixed_ref[:, lanes] = narrow[...]
    gated = query_ref[...].astype(F32) * mixed_ref[...]
    gated_ref[...] = gated.astype(BF16)
    turned_ref[...] = gated.T.astype(BF16)


def stack_arrived(*refs):
    stack_blocks(refs[:5], refs[5])


def weight_part(position_ref, turned_ref, own_ref, other_ref, out_ref, token_ref):
    place = position_ref[0]
    block = own_ref.shape[2]
    for ref, flip in ((own_ref, 0), (other_ref, 1)):
        for index, mask in enumerate(CHIP_MASKS):
            first = pl.multiple_of((place ^ (mask | flip)) * block, block)
            out_ref[:, pl.ds(first, block)] = jnp.dot(
                turned_ref[...], ref[index], preferred_element_type=F32
            ).astype(BF16)
    token_ref[...] = jnp.zeros(token_ref.shape, F32)


def project_rows(position_ref, query_ref, mixed_ref, gated_ref, out_weight_ref, own_ref, other_ref, query_grad_ref, drive_ref, sent_ref, mine_ref):
    place = position_ref[0]
    block = own_ref.shape[2]
    total = jnp.zeros(query_ref.shape, F32)
    for ref, flip, part_ref in ((other_ref, 1, sent_ref), (own_ref, 0, mine_ref)):
        for index, mask in enumerate(CHIP_MASKS):
            first = pl.multiple_of((place ^ (mask | flip)) * block, block)
            columns = out_weight_ref[:, pl.ds(first, block)]
            total = total + lax.dot_general(
                ref[index], columns, (((1,), (1,)), ((), ())), preferred_element_type=F32
            )
            part_ref[index] = jnp.dot(
                gated_ref[...], columns, preferred_element_type=F32
            ).astype(BF16)
    query_grad_ref[...] = (total * mixed_ref[...]).astype(BF16)
    drive_ref[...] = total * query_ref[...].astype(F32)


def backward_local(drive_ref, key_ref, value_ref, rate_ref, weight_ref, gain_ref, skip_ref, entering_ref, local_ref, sums_ref, product, carried):
    product[...] = key_ref[...].astype(F32) * value_ref[...].astype(F32)
    rates = rate_ref[...]
    weights = weight_ref[...]
    pole = jnp.exp(-rates)
    leap = jnp.exp(-float(SUB) * rates)
    state = jnp.zeros_like(rates)
    for block in reversed(range(SUB)):
        carried[pl.ds(block * SUB, SUB), :] = state
        inner = jnp.broadcast_to(drive_ref[pl.ds(block * SUB + SUB - 1, 1), :], rates.shape)
        for step in reversed(range(SUB - 1)):
            inner = pole * inner + drive_ref[pl.ds(block * SUB + step, 1), :]
        state = leap * state + inner
    sums_ref[pl.ds(0, SUB), :] = state
    sums_ref[pl.ds(SUB, SUB), :] = pole * entering_ref[...] * state
    sums_ref[pl.ds(2 * SUB, HALF), :] = jnp.zeros((HALF, LANES), F32)
    for half in range(2):
        drives = [strided(drive_ref, step, half) for step in range(SUB)]
        signal = [strided(product, step, half) for step in range(SUB)]
        totals = [skip_ref[...] * drive for drive in drives]
        direct = drives[0] * signal[0]
        for step in range(1, SUB):
            direct = direct + drives[step] * signal[step]
        sums_ref[pl.ds(2 * SUB, 1), :] += jnp.sum(direct, axis=0, keepdims=True)
        for mode in range(SUB):
            running = strided(carried, mode, half)
            gathered = jnp.zeros_like(running)
            for step in reversed(range(SUB)):
                running = pole[mode : mode + 1, :] * running + drives[step]
                totals[step] = totals[step] + weights[mode : mode + 1, :] * running
                gathered = gathered + signal[step] * running
            sums_ref[pl.ds(SUB + mode, 1), :] += jnp.sum(gathered, axis=0, keepdims=True)
        for step in range(SUB):
            local_ref[pl.ds(step + half * HALF * SUB, HALF, stride=SUB), :] = totals[step]
    sums_ref[pl.ds(SUB, SUB), :] *= gain_ref[...]


def backward_mix(position_ref, local_ref, key_ref, value_ref, rate_ref, weight_ref, inside_ref, whole_ref, first_ref, second_ref, third_ref, key_grad_ref, value_grad_ref, residue_ref, skip_sum_ref, scaled, grads):
    rates = rate_ref[...]
    tokens = local_ref.shape[0]
    across = [ref[pl.ds(0, SUB), :] for ref in (first_ref, second_ref, third_ref)]
    later = joined(True, tokens, position_ref, rates, inside_ref[...], across)
    pole = jnp.exp(-rates)
    power = weight_ref[...]
    for step in reversed(range(SUB)):
        power = power * pole
        scaled[pl.ds(step * SUB, SUB), :] = power
    for half in range(2):
        held = [
            block_decay(rates, mode, half, True) * later[mode : mode + 1, :] for mode in range(SUB)
        ]
        for step in range(SUB):
            total = strided(local_ref, step, half)
            for mode in range(SUB):
                total = total + scaled[pl.ds(step * SUB + mode, 1), :] * held[mode]
            grads[pl.ds(step + half * HALF * SUB, HALF, stride=SUB), :] = total
    product_grad = grads[...]
    key_grad_ref[...] = (product_grad * value_ref[...].astype(F32)).astype(BF16)
    value_grad_ref[...] = (product_grad * key_ref[...].astype(F32)).astype(BF16)
    for first, count, ref in ((SUB, SUB, residue_ref), (2 * SUB, 1, skip_sum_ref)):
        part = pl.ds(first, count)
        ref[...] = (whole_ref[part, :] + first_ref[part, :]) + (
            second_ref[part, :] + third_ref[part, :]
        )


def widened(ref, *place):
    return ref[place].astype(F32) if place else ref[...].astype(F32)


def merge_cores(mine_ref, other_ref, even_ref, odd_ref, rest_ref):
    for index, mask in enumerate(CHIP_MASKS):
        total = (widened(mine_ref, index) + widened(other_ref, index)).astype(BF16)
        if mask == 8:
            even_ref[...] = total
        elif mask == 10:
            odd_ref[...] = total
        else:
            rest_ref[index if mask < 8 else index - 2] = total


def merge_far(rest_ref, even_ref, odd_ref, first_ref, third_ref):
    first_ref[0] = rest_ref[2]
    first_ref[1] = (widened(rest_ref, 3) + widened(odd_ref)).astype(BF16)
    third_ref[0] = (widened(rest_ref, 4) + widened(even_ref)).astype(BF16)
    third_ref[1] = rest_ref[5]


def backward_near(tokens, position_ref, rate_ref, *rest):
    near_sums(True, tokens, position_ref, rate_ref, rest[:4], rest[4], rest[5])


def merge_near(rest_ref, first_ref, third_ref, kept_ref, sent_ref):
    for index, ref in enumerate((kept_ref, sent_ref)):
        total = widened(rest_ref, index) + widened(first_ref, index) + widened(third_ref, index)
        ref[...] = total.astype(ref.dtype)


def merge_last(kept_ref, arrived_ref, out_ref):
    out_ref[...] = (kept_ref[...] + widened(arrived_ref)).astype(BF16)


VMEM = pl.BlockSpec(memory_space=pltpu.VMEM)
SMEM = pl.BlockSpec(memory_space=pltpu.SMEM)
ANY = pl.BlockSpec(memory_space=pl.ANY)


def tile_of(rows):
    return pl.BlockSpec((rows, LANES), lambda tile: (0, tile))


def shape_of(rows, columns, kind=F32):
    return jax.ShapeDtypeStruct((rows, columns), kind)


def ordered_call(body, ordered, in_specs, *operands, **options):
    count = len(ordered)

    def skipping(*refs):
        body(*refs[count:])

    return pl.pallas_call(skipping, in_specs=[ANY] * count + in_specs, **options)(
        *ordered, *operands
    )


def granted(mebibytes):
    return pltpu.CompilerParams(vmem_limit_bytes=mebibytes * 1024 * 1024)


def kind_of(*shape, dtype=BF16):
    return jax.ShapeDtypeStruct(shape, dtype)


def local_call(body, out_shape, *operands, ordered=(), scalars=0, scratch=(), limit=11):
    plain = body.func if isinstance(body, functools.partial) else body
    return ordered_call(
        body,
        ordered,
        [SMEM] * scalars
        + [VMEM] * (len(operands) - scalars),
        *operands,
        out_specs=[VMEM] * len(out_shape),
        out_shape=out_shape,
        scratch_shapes=scratch,
        compiler_params=granted(limit),
        name=plain.__name__,
    )


def on_device(query_rows, key_rows, value_rows, residues, decays, skip_gain, out_weight, cotangent):
    tokens, width = query_rows.shape
    modes = residues.shape[0]
    ctx_count = lax.axis_size("ctx")
    chan_count = lax.axis_size("chan")
    positions = jnp.stack([lax.axis_index("chan"), lax.axis_index("ctx")]).astype(jnp.int32)
    rates = decays / (tokens * ctx_count)
    gains = jnp.sqrt(-jnp.expm1(-2.0 * rates) / modes)
    weights = residues * gains
    skip_row = skip_gain.reshape(1, width)
    tiles = width // LANES
    rows = tile_of(tokens)
    few = tile_of(modes)
    one = tile_of(1)
    tall = 2 * modes + HALF
    sums = tile_of(tall)
    block_scratch = pltpu.VMEM((tokens, LANES), F32)
    columns = cotangent.shape[1]
    block = kind_of(tokens, columns)
    pair_block = kind_of(2, tokens, columns)
    eight = kind_of(8, tokens, columns)
    square = shape_of(tokens, width)
    state_shape = shape_of(modes, width)
    tall_shape = shape_of(tall, width)

    arrived = traded(cotangent, "chan", 2)
    state, local = pl.pallas_call(
        forward_local,
        grid=(tiles,),
        in_specs=[rows, rows, few, few, one],
        out_specs=[few, rows],
        out_shape=[state_shape, square],
        scratch_shapes=[block_scratch] * 3,
        name="forward_local",
    )(key_rows, value_rows, rates, weights, skip_row)
    near = [state] + [traded(state, "ctx", mask) for mask in (1, 2, 3)]
    inside, whole, pair = local_call(
        functools.partial(forward_near, tokens),
        [state_shape, state_shape, pair_block],
        positions,
        rates,
        *near,
        cotangent,
        arrived,
        scalars=1,
    )

    first, third = traded(pair, "chan", 4), traded(pair, "chan", 12)
    across = [traded(whole, "ctx", 4 * mask) for mask in (1, 2, 3)]
    far = local_call(open_far, [block, block], first, third, ordered=across)
    mixed, gated, gated_turned, entering = local_call(
        forward_mix,
        [square, kind_of(tokens, width), kind_of(width, tokens), state_shape],
        positions,
        local,
        query_rows,
        rates,
        weights,
        inside,
        *across,
        ordered=far[:1],
        scalars=1,
        scratch=[block_scratch] * 2,
    )

    even, odd = traded(far[0], "chan", 12), traded(far[1], "chan", 4)
    own = local_call(stack_arrived, [eight], pair, first, third, even, odd)[0]

    sibling = traded(own, "chan", 1)
    weight_share, token = local_call(
        weight_part,
        [kind_of(width, chan_count * columns), shape_of(HALF, LANES)],
        positions,
        gated_turned,
        own,
        sibling,
        scalars=1,
    )
    weight_grad = lax.psum_scatter(weight_share, "ctx", scatter_dimension=1, tiled=True)
    query_grad, drive, other, mine = local_call(
        project_rows,
        [kind_of(tokens, width), square, eight, eight],
        positions,
        query_rows,
        mixed,
        gated,
        out_weight,
        own,
        sibling,
        ordered=[token],
        scalars=1,
        limit=14,
    )
    back_local, back_state = pl.pallas_call(
        backward_local,
        grid=(tiles,),
        in_specs=[rows, rows, rows, few, few, few, one, few],
        out_specs=[rows, sums],
        out_shape=[square, tall_shape],
        scratch_shapes=[block_scratch] * 2,
        name="backward_local",
    )(drive, key_rows, value_rows, rates, weights, gains, skip_row, entering)
    even, odd, rest = local_call(
        merge_cores,
        [block, block, kind_of(6, tokens, columns)],
        mine,
        traded(other, "chan", 1),
        ordered=[back_state],
    )

    near = [back_state] + [traded(back_state, "ctx", mask) for mask in (1, 2, 3)]
    inside, whole = local_call(
        functools.partial(backward_near, tokens),
        [state_shape, tall_shape],
        positions,
        rates,
        *near,
        scalars=1,
    )
    first, third = local_call(
        merge_far,
        [pair_block, pair_block],
        rest,
        traded(even, "chan", 4),
        traded(odd, "chan", 12),
        ordered=[whole],
    )

    across = [traded(whole, "ctx", 4 * mask) for mask in (1, 2, 3)]
    kept, sent = local_call(
        merge_near,
        [shape_of(tokens, columns), block],
        rest,
        traded(first, "chan", 4),
        traded(third, "chan", 12),
        ordered=across,
    )

    layer_out = local_call(
        merge_last, [kind_of(tokens, columns)], kept, traded(sent, "chan", 2)
    )[0]
    key_grad, value_grad, residue_grad, skip_sum = pl.pallas_call(
        backward_mix,
        grid=(tiles,),
        in_specs=[SMEM, rows, rows, rows, few, few, few] + [sums] * 4,
        out_specs=[rows, rows, few, one],
        out_shape=[
            kind_of(tokens, width),
            kind_of(tokens, width),
            state_shape,
            shape_of(1, width),
        ],
        scratch_shapes=[block_scratch] * 2,
        name="backward_mix",
    )(positions, back_local, key_rows, value_rows, rates, weights, inside, whole, *across)
    return (
        layer_out,
        query_grad,
        key_grad,
        value_grad,
        residue_grad,
        skip_sum.reshape(width),
        weight_grad.astype(F32),
    )


def solution(mesh):
    placed = (
        P("ctx", "chan"),
        P("ctx", "chan"),
        P("ctx", "chan"),
        P(None, "chan"),
        P(None, "chan"),
        P("chan"),
        P("chan", None),
        P("ctx", "chan"),
    )
    return jax.shard_map(
        on_device,
        mesh=mesh,
        in_specs=placed,
        out_specs=(
            P("ctx", "chan"),
            P("ctx", "chan"),
            P("ctx", "chan"),
            P("ctx", "chan"),
            P(None, "chan"),
            P("chan"),
            P("chan", "ctx"),
        ),
        check_vma=False,
    )
```

```python
import functools

import jax
import jax.numpy as jnp
from jax import lax
from jax.experimental import pallas as pl
from jax.experimental.pallas import tpu as pltpu
from jax.sharding import PartitionSpec as P

F32 = jnp.float32
BF16 = jnp.bfloat16
LANES = 128
SUB = 16
HALF = 8
CHIP_MASKS = tuple(range(0, 16, 2))


def traded(value, axis, mask):
    pairs = [(source, source ^ mask) for source in range(lax.axis_size(axis))]
    return lax.ppermute(value, axis, pairs)


def strided(ref, offset, half):
    return ref[pl.ds(offset + half * HALF * SUB, HALF, stride=SUB), :]


def shortfall(value):
    series = jnp.ones_like(value)
    for order in range(10, 1, -1):
        series = 1.0 - value * (1.0 / order) * series
    return jnp.where(value < 0.5, value * series, 1.0 - jnp.exp(-value))


def forward_local(length, key_ref, value_ref, decay_ref, residue_ref, skip_ref, state_ref, mixed_ref, rate_ref, gain_ref, weight_ref, product, carried, scaled):
    product[...] = key_ref[...].astype(F32) * value_ref[...].astype(F32)
    rates = decay_ref[...] * (1.0 / length)
    gains = jnp.sqrt(shortfall(2.0 * rates) * (1.0 / rates.shape[0]))
    weights = residue_ref[...] * gains
    rate_ref[...] = rates
    gain_ref[...] = gains
    weight_ref[...] = weights
    pole = jnp.exp(-rates)
    leap = jnp.exp(-float(SUB) * rates)
    state = jnp.zeros_like(rates)
    for block in range(SUB):
        carried[pl.ds(block * SUB, SUB), :] = state
        inner = jnp.broadcast_to(product[pl.ds(block * SUB, 1), :], rates.shape)
        for step in range(1, SUB):
            inner = pole * inner + product[pl.ds(block * SUB + step, 1), :]
        state = leap * state + inner
    state_ref[...] = state
    taps = []
    power = weights
    for step in range(SUB):
        taps.append(jnp.sum(power, axis=0, keepdims=True))
        power = power * pole
        scaled[pl.ds(step * SUB, SUB), :] = power
    taps[0] = taps[0] + skip_ref[...]
    for half in range(2):
        held = [strided(carried, mode, half) for mode in range(SUB)]
        signal = [strided(product, step, half) for step in range(SUB)]
        for step in range(SUB):
            total = taps[0] * signal[step]
            for lag in range(1, step + 1):
                total = total + taps[lag] * signal[step - lag]
            for mode in range(SUB):
                total = total + scaled[pl.ds(step * SUB + mode, 1), :] * held[mode]
            mixed_ref[pl.ds(step + half * HALF * SUB, HALF, stride=SUB), :] = total


def block_decay(rates, mode, half, backward):
    place = lax.broadcasted_iota(jnp.int32, (HALF, LANES), 0).astype(F32) + float(half * HALF)
    distance = float(SUB - 1) - place if backward else place
    return jnp.exp(-float(SUB) * distance * rates[mode : mode + 1, :])


def falling(rates, distance):
    reach = jnp.maximum(distance, 0).astype(F32)
    present = jnp.where(distance >= 0, 1.0, 0.0).astype(F32)
    return jnp.exp(-reach * rates) * present


def near_sums(backward, tokens, position_ref, rate_ref, value_refs, inside_ref, whole_ref):
    values = [ref[...] for ref in value_refs]
    rates = rate_ref[...]
    modes = rates.shape[0]
    low = position_ref[1] & 3
    inside = jnp.zeros_like(rates)
    whole = jnp.zeros_like(rates)
    for mask in range(4):
        spot = low ^ mask
        state = values[mask][:modes]
        gap = spot - low - 1 if backward else low - 1 - spot
        far = spot if backward else 3 - spot
        inside = inside + falling(rates, tokens * gap) * state
        whole = whole + falling(rates, tokens * far) * state
    inside_ref[...] = inside
    whole_ref[pl.ds(0, modes), :] = whole
    if values[0].shape[0] > modes:
        sums = [value[modes:] for value in values]
        whole_ref[pl.ds(modes, sums[0].shape[0]), :] = (sums[0] + sums[1]) + (sums[2] + sums[3])


def forward_near(tokens, position_ref, rate_ref, *rest):
    own_ref, arrived_ref, inside_ref, whole_ref, pair_ref = rest[4:]
    near_sums(False, tokens, position_ref, rate_ref, rest[:4], inside_ref, whole_ref)
    pair_ref[0] = own_ref[...]
    pair_ref[1] = arrived_ref[...]


def open_far(first_ref, third_ref, even_ref, odd_ref):
    even_ref[...] = first_ref[0]
    odd_ref[...] = third_ref[1]


def stack_blocks(refs, out_ref):
    pair, first, third, even, odd = refs
    for index, block in enumerate((pair.at[0], pair.at[1], first.at[0], first.at[1])):
        out_ref[index] = block[...]
    for index, block in enumerate((even, odd, third.at[0], third.at[1])):
        out_ref[4 + index] = block[...]


def joined(backward, tokens, position_ref, rates, inside, across):
    low = position_ref[1] & 3
    high = lax.shift_right_logical(position_ref[1], 2)
    total = jnp.zeros_like(rates)
    for mask in range(1, 4):
        spot = high ^ mask
        gap = spot - high - 1 if backward else high - 1 - spot
        total = total + falling(rates, 4 * tokens * gap) * across[mask - 1]
    span = 3 - low if backward else low
    return inside + falling(rates, tokens * span) * total


def forward_mix(position_ref, local_ref, query_ref, rate_ref, weight_ref, inside_ref, first_ref, second_ref, third_ref, mixed_ref, gated_ref, turned_ref, entering_ref, scaled, narrow):
    tokens = local_ref.shape[0]
    for tile in range(2):
        lanes = pl.ds(tile * LANES, LANES)
        narrow[...] = local_ref[:, lanes]
        rates = rate_ref[:, lanes]
        weights = weight_ref[:, lanes]
        across = [ref[:, lanes] for ref in (first_ref, second_ref, third_ref)]
        entering = joined(False, tokens, position_ref, rates, inside_ref[:, lanes], across)
        entering_ref[:, lanes] = entering
        pole = jnp.exp(-rates)
        power = weights
        for step in range(SUB):
            power = power * pole
            scaled[pl.ds(step * SUB, SUB), :] = power
        for half in range(2):
            held = [
                block_decay(rates, mode, half, False) * entering[mode : mode + 1, :]
                for mode in range(SUB)
            ]
            for step in range(SUB):
                rows = pl.ds(step + half * HALF * SUB, HALF, stride=SUB)
                total = narrow[rows, :]
                for mode in range(SUB):
                    total = total + scaled[pl.ds(step * SUB + mode, 1), :] * held[mode]
                narrow[rows, :] = total
        mixed_ref[:, lanes] = narrow[...]
    gated = query_ref[...].astype(F32) * mixed_ref[...]
    gated_ref[...] = gated.astype(BF16)
    turned_ref[...] = gated.T.astype(BF16)


def stack_arrived(*refs):
    stack_blocks(refs[:5], refs[5])


def weight_part(position_ref, turned_ref, own_ref, other_ref, out_ref, token_ref):
    place = position_ref[0]
    for ref, flip in ((own_ref, 0), (other_ref, 1)):
        for index, mask in enumerate(CHIP_MASKS):
            target = place ^ (mask | flip)
            out_ref[target & 7, lax.shift_right_logical(target, 3)] = jnp.dot(
                turned_ref[...], ref[index], preferred_element_type=F32
            ).astype(BF16)
    token_ref[...] = jnp.zeros(token_ref.shape, F32)


def project_rows(position_ref, query_ref, mixed_ref, gated_ref, out_weight_ref, own_ref, other_ref, query_grad_ref, drive_ref, sent_ref, mine_ref):
    place = position_ref[0]
    block = own_ref.shape[2]
    total = jnp.zeros(query_ref.shape, F32)
    for ref, flip, part_ref in ((other_ref, 1, sent_ref), (own_ref, 0, mine_ref)):
        for index, mask in enumerate(CHIP_MASKS):
            first = pl.multiple_of((place ^ (mask | flip)) * block, block)
            columns = out_weight_ref[:, pl.ds(first, block)]
            total = total + lax.dot_general(
                ref[index], columns, (((1,), (1,)), ((), ())), preferred_element_type=F32
            )
            part_ref[index] = jnp.dot(
                gated_ref[...], columns, preferred_element_type=F32
            ).astype(BF16)
    query_grad_ref[...] = (total * mixed_ref[...]).astype(BF16)
    drive_ref[...] = total * query_ref[...].astype(F32)


def backward_local(drive_ref, key_ref, value_ref, rate_ref, weight_ref, gain_ref, skip_ref, entering_ref, local_ref, sums_ref, product, carried):
    product[...] = key_ref[...].astype(F32) * value_ref[...].astype(F32)
    rates = rate_ref[...]
    weights = weight_ref[...]
    pole = jnp.exp(-rates)
    leap = jnp.exp(-float(SUB) * rates)
    state = jnp.zeros_like(rates)
    for block in reversed(range(SUB)):
        carried[pl.ds(block * SUB, SUB), :] = state
        inner = jnp.broadcast_to(drive_ref[pl.ds(block * SUB + SUB - 1, 1), :], rates.shape)
        for step in reversed(range(SUB - 1)):
            inner = pole * inner + drive_ref[pl.ds(block * SUB + step, 1), :]
        state = leap * state + inner
    sums_ref[pl.ds(0, SUB), :] = state
    sums_ref[pl.ds(SUB, SUB), :] = pole * entering_ref[...] * state
    sums_ref[pl.ds(2 * SUB, HALF), :] = jnp.zeros((HALF, LANES), F32)
    for half in range(2):
        drives = [strided(drive_ref, step, half) for step in range(SUB)]
        signal = [strided(product, step, half) for step in range(SUB)]
        totals = [skip_ref[...] * drive for drive in drives]
        direct = drives[0] * signal[0]
        for step in range(1, SUB):
            direct = direct + drives[step] * signal[step]
        sums_ref[pl.ds(2 * SUB, 1), :] += jnp.sum(direct, axis=0, keepdims=True)
        for mode in range(SUB):
            running = strided(carried, mode, half)
            gathered = jnp.zeros_like(running)
            for step in reversed(range(SUB)):
                running = pole[mode : mode + 1, :] * running + drives[step]
                totals[step] = totals[step] + weights[mode : mode + 1, :] * running
                gathered = gathered + signal[step] * running
            sums_ref[pl.ds(SUB + mode, 1), :] += jnp.sum(gathered, axis=0, keepdims=True)
        for step in range(SUB):
            local_ref[pl.ds(step + half * HALF * SUB, HALF, stride=SUB), :] = totals[step]
    sums_ref[pl.ds(SUB, SUB), :] *= gain_ref[...]


def backward_mix(position_ref, local_ref, key_ref, value_ref, rate_ref, weight_ref, inside_ref, whole_ref, first_ref, second_ref, third_ref, key_grad_ref, value_grad_ref, residue_ref, skip_sum_ref, scaled, grads):
    rates = rate_ref[...]
    tokens = local_ref.shape[0]
    across = [ref[pl.ds(0, SUB), :] for ref in (first_ref, second_ref, third_ref)]
    later = joined(True, tokens, position_ref, rates, inside_ref[...], across)
    pole = jnp.exp(-rates)
    power = weight_ref[...]
    for step in reversed(range(SUB)):
        power = power * pole
        scaled[pl.ds(step * SUB, SUB), :] = power
    for half in range(2):
        held = [
            block_decay(rates, mode, half, True) * later[mode : mode + 1, :] for mode in range(SUB)
        ]
        for step in range(SUB):
            total = strided(local_ref, step, half)
            for mode in range(SUB):
                total = total + scaled[pl.ds(step * SUB + mode, 1), :] * held[mode]
            grads[pl.ds(step + half * HALF * SUB, HALF, stride=SUB), :] = total
    product_grad = grads[...]
    key_grad_ref[...] = (product_grad * value_ref[...].astype(F32)).astype(BF16)
    value_grad_ref[...] = (product_grad * key_ref[...].astype(F32)).astype(BF16)
    for first, count, ref in ((SUB, SUB, residue_ref), (2 * SUB, 1, skip_sum_ref)):
        part = pl.ds(first, count)
        ref[...] = (whole_ref[part, :] + first_ref[part, :]) + (
            second_ref[part, :] + third_ref[part, :]
        )


def widened(ref, *place):
    return ref[place].astype(F32) if place else ref[...].astype(F32)


def merge_cores(mine_ref, other_ref, even_ref, odd_ref, rest_ref):
    for index, mask in enumerate(CHIP_MASKS):
        total = (widened(mine_ref, index) + widened(other_ref, index)).astype(BF16)
        if mask == 8:
            even_ref[...] = total
        elif mask == 10:
            odd_ref[...] = total
        else:
            rest_ref[index if mask < 8 else index - 2] = total


def merge_far(rest_ref, even_ref, odd_ref, first_ref, third_ref):
    first_ref[0] = rest_ref[2]
    first_ref[1] = (widened(rest_ref, 3) + widened(odd_ref)).astype(BF16)
    third_ref[0] = (widened(rest_ref, 4) + widened(even_ref)).astype(BF16)
    third_ref[1] = rest_ref[5]


def backward_near(tokens, position_ref, rate_ref, *rest):
    near_sums(True, tokens, position_ref, rate_ref, rest[:4], rest[4], rest[5])


def merge_near(rest_ref, first_ref, third_ref, kept_ref, sent_ref):
    for index, ref in enumerate((kept_ref, sent_ref)):
        total = widened(rest_ref, index) + widened(first_ref, index) + widened(third_ref, index)
        ref[...] = total.astype(ref.dtype)


def join_weight(position_ref, kept_ref, arrived_ref, out_ref):
    side = lax.shift_right_logical(position_ref[1], 3)
    out_ref[...] = kept_ref[side].astype(F32) + widened(arrived_ref)


def merge_last(kept_ref, arrived_ref, out_ref):
    out_ref[...] = (kept_ref[...] + widened(arrived_ref)).astype(BF16)


VMEM = pl.BlockSpec(memory_space=pltpu.VMEM)
SMEM = pl.BlockSpec(memory_space=pltpu.SMEM)
ANY = pl.BlockSpec(memory_space=pl.ANY)


def tile_of(rows):
    return pl.BlockSpec((rows, LANES), lambda tile: (0, tile))


def shape_of(rows, columns, kind=F32):
    return jax.ShapeDtypeStruct((rows, columns), kind)


def ordered_call(body, ordered, in_specs, *operands, **options):
    count = len(ordered)

    def skipping(*refs):
        body(*refs[count:])

    return pl.pallas_call(skipping, in_specs=[ANY] * count + in_specs, **options)(
        *ordered, *operands
    )


def granted(mebibytes):
    return pltpu.CompilerParams(vmem_limit_bytes=mebibytes * 1024 * 1024)


def kind_of(*shape, dtype=BF16):
    return jax.ShapeDtypeStruct(shape, dtype)


def local_call(body, out_shape, *operands, ordered=(), scalars=0, scratch=(), limit=11):
    plain = body.func if isinstance(body, functools.partial) else body
    return ordered_call(
        body,
        ordered,
        [SMEM] * scalars
        + [VMEM] * (len(operands) - scalars),
        *operands,
        out_specs=[VMEM] * len(out_shape),
        out_shape=out_shape,
        scratch_shapes=scratch,
        compiler_params=granted(limit),
        name=plain.__name__,
    )


def on_device(query_rows, key_rows, value_rows, residues, decays, skip_gain, out_weight, cotangent):
    tokens, width = query_rows.shape
    modes = residues.shape[0]
    ctx_count = lax.axis_size("ctx")
    chan_count = lax.axis_size("chan")
    positions = jnp.stack([lax.axis_index("chan"), lax.axis_index("ctx")]).astype(jnp.int32)
    skip_row = skip_gain.reshape(1, width)
    tiles = width // LANES
    rows = tile_of(tokens)
    few = tile_of(modes)
    one = tile_of(1)
    tall = 2 * modes + HALF
    sums = tile_of(tall)
    block_scratch = pltpu.VMEM((tokens, LANES), F32)
    columns = cotangent.shape[1]
    block = kind_of(tokens, columns)
    pair_block = kind_of(2, tokens, columns)
    eight = kind_of(8, tokens, columns)
    square = shape_of(tokens, width)
    state_shape = shape_of(modes, width)
    tall_shape = shape_of(tall, width)

    arrived = traded(cotangent, "chan", 2)
    state, local, rates, gains, weights = pl.pallas_call(
        functools.partial(forward_local, tokens * ctx_count),
        grid=(tiles,),
        in_specs=[rows, rows, few, few, one],
        out_specs=[few, rows, few, few, few],
        out_shape=[state_shape, square, state_shape, state_shape, state_shape],
        scratch_shapes=[block_scratch] * 3,
        name="forward_local",
    )(key_rows, value_rows, decays, residues, skip_row)
    near = [state] + [traded(state, "ctx", mask) for mask in (1, 2, 3)]
    inside, whole, pair = local_call(
        functools.partial(forward_near, tokens),
        [state_shape, state_shape, pair_block],
        positions,
        rates,
        *near,
        cotangent,
        arrived,
        scalars=1,
    )

    first, third = traded(pair, "chan", 4), traded(pair, "chan", 12)
    across = [traded(whole, "ctx", 4 * mask) for mask in (1, 2, 3)]
    far = local_call(open_far, [block, block], first, third, ordered=across)
    mixed, gated, gated_turned, entering = local_call(
        forward_mix,
        [square, kind_of(tokens, width), kind_of(width, tokens), state_shape],
        positions,
        local,
        query_rows,
        rates,
        weights,
        inside,
        *across,
        ordered=far[:1],
        scalars=1,
        scratch=[block_scratch] * 2,
    )

    even, odd = traded(far[0], "chan", 12), traded(far[1], "chan", 4)
    own = local_call(stack_arrived, [eight], pair, first, third, even, odd)[0]

    sibling = traded(own, "chan", 1)
    weight_share, token = local_call(
        weight_part,
        [kind_of(8, 2, width, columns), shape_of(HALF, LANES)],
        positions,
        gated_turned,
        own,
        sibling,
        scalars=1,
    )
    weight_grad = lax.psum_scatter(
        weight_share,
        "ctx",
        scatter_dimension=0,
        axis_index_groups=[list(range(8)), list(range(8, 16))],
        tiled=False,
    )
    query_grad, drive, other, mine = local_call(
        project_rows,
        [kind_of(tokens, width), square, eight, eight],
        positions,
        query_rows,
        mixed,
        gated,
        out_weight,
        own,
        sibling,
        ordered=[token],
        scalars=1,
        limit=14,
    )
    back_local, back_state = pl.pallas_call(
        backward_local,
        grid=(tiles,),
        in_specs=[rows, rows, rows, few, few, few, one, few],
        out_specs=[rows, sums],
        out_shape=[square, tall_shape],
        scratch_shapes=[block_scratch] * 2,
        name="backward_local",
    )(drive, key_rows, value_rows, rates, weights, gains, skip_row, entering)
    even, odd, rest = local_call(
        merge_cores,
        [block, block, kind_of(6, tokens, columns)],
        mine,
        traded(other, "chan", 1),
        ordered=[back_state],
    )

    near = [back_state] + [traded(back_state, "ctx", mask) for mask in (1, 2, 3)]
    inside, whole = local_call(
        functools.partial(backward_near, tokens),
        [state_shape, tall_shape],
        positions,
        rates,
        *near,
        scalars=1,
    )
    first, third = local_call(
        merge_far,
        [pair_block, pair_block],
        rest,
        traded(even, "chan", 4),
        traded(odd, "chan", 12),
        ordered=[whole],
    )

    across = [traded(whole, "ctx", 4 * mask) for mask in (1, 2, 3)]
    kept, sent = local_call(
        merge_near,
        [shape_of(tokens, columns), block],
        rest,
        traded(first, "chan", 4),
        traded(third, "chan", 12),
        ordered=across,
    )

    layer_out = local_call(
        merge_last, [kind_of(tokens, columns)], kept, traded(sent, "chan", 2)
    )[0]
    key_grad, value_grad, residue_grad, skip_sum = pl.pallas_call(
        backward_mix,
        grid=(tiles,),
        in_specs=[SMEM, rows, rows, rows, few, few, few] + [sums] * 4,
        out_specs=[rows, rows, few, one],
        out_shape=[
            kind_of(tokens, width),
            kind_of(tokens, width),
            state_shape,
            shape_of(1, width),
        ],
        scratch_shapes=[block_scratch] * 2,
        name="backward_mix",
    )(positions, back_local, key_rows, value_rows, rates, weights, inside, whole, *across)
    side = lax.axis_index("ctx") >> 3
    whole_of = lambda *shape: pl.BlockSpec(shape, lambda step: (0,) * len(shape))
    weight_grad = pl.pallas_call(
        join_weight,
        grid=(1,),
        in_specs=[SMEM, whole_of(2, width, columns), whole_of(width, columns)],
        out_specs=whole_of(width, columns),
        out_shape=shape_of(width, columns),
        name="join_weight",
    )(
        positions,
        weight_grad,
        traded(lax.dynamic_index_in_dim(weight_grad, 1 - side, 0, keepdims=False), "ctx", 8),
    )
    return (
        layer_out,
        query_grad,
        key_grad,
        value_grad,
        residue_grad,
        skip_sum.reshape(width),
        weight_grad,
    )


def solution(mesh):
    placed = (
        P("ctx", "chan"),
        P("ctx", "chan"),
        P("ctx", "chan"),
        P(None, "chan"),
        P(None, "chan"),
        P("chan"),
        P("chan", None),
        P("ctx", "chan"),
    )
    return jax.shard_map(
        on_device,
        mesh=mesh,
        in_specs=placed,
        out_specs=(
            P("ctx", "chan"),
            P("ctx", "chan"),
            P("ctx", "chan"),
            P("ctx", "chan"),
            P(None, "chan"),
            P("chan"),
            P("chan", "ctx"),
        ),
        check_vma=False,
    )
```

```python
import functools

import jax
import jax.numpy as jnp
from jax import lax
from jax.experimental import pallas as pl
from jax.experimental.pallas import tpu as pltpu
from jax.sharding import PartitionSpec as P

F32 = jnp.float32
BF16 = jnp.bfloat16
LANES = 128
SUB = 16
HALF = 8
CHIP_MASKS = tuple(range(0, 16, 2))


def traded(value, axis, mask):
    pairs = [(source, source ^ mask) for source in range(lax.axis_size(axis))]
    return lax.ppermute(value, axis, pairs)


def strided(ref, offset, half):
    return ref[pl.ds(offset + half * HALF * SUB, HALF, stride=SUB), :]


def shortfall(value):
    series = jnp.ones_like(value)
    for order in range(10, 1, -1):
        series = 1.0 - value * (1.0 / order) * series
    return jnp.where(value < 0.5, value * series, 1.0 - jnp.exp(-value))


def forward_local(length, key_ref, value_ref, decay_ref, residue_ref, skip_ref, state_ref, mixed_ref, rate_ref, gain_ref, weight_ref, product, carried, scaled):
    product[...] = key_ref[...].astype(F32) * value_ref[...].astype(F32)
    rates = decay_ref[...] * (1.0 / length)
    gains = jnp.sqrt(shortfall(2.0 * rates) * (1.0 / rates.shape[0]))
    weights = residue_ref[...] * gains
    rate_ref[...] = rates
    gain_ref[...] = gains
    weight_ref[...] = weights
    pole = jnp.exp(-rates)
    leap = jnp.exp(-float(SUB) * rates)
    state = jnp.zeros_like(rates)
    for block in range(SUB):
        carried[pl.ds(block * SUB, SUB), :] = state
        inner = jnp.broadcast_to(product[pl.ds(block * SUB, 1), :], rates.shape)
        for step in range(1, SUB):
            inner = pole * inner + product[pl.ds(block * SUB + step, 1), :]
        state = leap * state + inner
    state_ref[pl.ds(0, SUB), :] = state
    state_ref[pl.ds(SUB, SUB), :] = rates
    taps = []
    power = weights
    for step in range(SUB):
        taps.append(jnp.sum(power, axis=0, keepdims=True))
        power = power * pole
        scaled[pl.ds(step * SUB, SUB), :] = power
    taps[0] = taps[0] + skip_ref[...]
    for half in range(2):
        held = [strided(carried, mode, half) for mode in range(SUB)]
        signal = [strided(product, step, half) for step in range(SUB)]
        for step in range(SUB):
            total = taps[0] * signal[step]
            for lag in range(1, step + 1):
                total = total + taps[lag] * signal[step - lag]
            for mode in range(SUB):
                total = total + scaled[pl.ds(step * SUB + mode, 1), :] * held[mode]
            mixed_ref[pl.ds(step + half * HALF * SUB, HALF, stride=SUB), :] = total


def block_decay(rates, mode, half, backward):
    place = lax.broadcasted_iota(jnp.int32, (HALF, LANES), 0).astype(F32) + float(half * HALF)
    distance = float(SUB - 1) - place if backward else place
    return jnp.exp(-float(SUB) * distance * rates[mode : mode + 1, :])


def falling(rates, distance):
    reach = jnp.maximum(distance, 0).astype(F32)
    present = jnp.where(distance >= 0, 1.0, 0.0).astype(F32)
    return jnp.exp(-reach * rates) * present


def near_sums(backward, tokens, position_ref, rates, values, inside_ref, whole_ref):
    modes = rates.shape[0]
    low = position_ref[1] & 3
    inside = jnp.zeros_like(rates)
    whole = jnp.zeros_like(rates)
    for mask in range(4):
        spot = low ^ mask
        state = values[mask][:modes]
        gap = spot - low - 1 if backward else low - 1 - spot
        far = spot if backward else 3 - spot
        inside = inside + falling(rates, tokens * gap) * state
        whole = whole + falling(rates, tokens * far) * state
    inside_ref[...] = inside
    whole_ref[pl.ds(0, modes), :] = whole
    if backward:
        sums = [value[modes:] for value in values]
        whole_ref[pl.ds(modes, sums[0].shape[0]), :] = (sums[0] + sums[1]) + (sums[2] + sums[3])


def forward_near(tokens, position_ref, *rest):
    own_ref, arrived_ref, inside_ref, whole_ref, pair_ref = rest[4:]
    values = [ref[...] for ref in rest[:4]]
    rates = values[0][values[0].shape[0] // 2 :]
    near_sums(False, tokens, position_ref, rates, values, inside_ref, whole_ref)
    pair_ref[0] = own_ref[...]
    pair_ref[1] = arrived_ref[...]


def open_far(first_ref, third_ref, even_ref, odd_ref):
    even_ref[...] = first_ref[0]
    odd_ref[...] = third_ref[1]


def stack_blocks(refs, out_ref):
    pair, first, third, even, odd = refs
    for index, block in enumerate((pair.at[0], pair.at[1], first.at[0], first.at[1])):
        out_ref[index] = block[...]
    for index, block in enumerate((even, odd, third.at[0], third.at[1])):
        out_ref[4 + index] = block[...]


def joined(backward, tokens, position_ref, rates, inside, across):
    low = position_ref[1] & 3
    high = lax.shift_right_logical(position_ref[1], 2)
    total = jnp.zeros_like(rates)
    for mask in range(1, 4):
        spot = high ^ mask
        gap = spot - high - 1 if backward else high - 1 - spot
        total = total + falling(rates, 4 * tokens * gap) * across[mask - 1]
    span = 3 - low if backward else low
    return inside + falling(rates, tokens * span) * total


def forward_mix(position_ref, local_ref, query_ref, rate_ref, weight_ref, inside_ref, first_ref, second_ref, third_ref, mixed_ref, gated_ref, turned_ref, entering_ref, scaled, narrow):
    tokens = local_ref.shape[0]
    for tile in range(2):
        lanes = pl.ds(tile * LANES, LANES)
        narrow[...] = local_ref[:, lanes]
        rates = rate_ref[:, lanes]
        weights = weight_ref[:, lanes]
        across = [ref[:, lanes] for ref in (first_ref, second_ref, third_ref)]
        entering = joined(False, tokens, position_ref, rates, inside_ref[:, lanes], across)
        entering_ref[:, lanes] = entering
        pole = jnp.exp(-rates)
        power = weights
        for step in range(SUB):
            power = power * pole
            scaled[pl.ds(step * SUB, SUB), :] = power
        for half in range(2):
            held = [
                block_decay(rates, mode, half, False) * entering[mode : mode + 1, :]
                for mode in range(SUB)
            ]
            for step in range(SUB):
                rows = pl.ds(step + half * HALF * SUB, HALF, stride=SUB)
                total = narrow[rows, :]
                for mode in range(SUB):
                    total = total + scaled[pl.ds(step * SUB + mode, 1), :] * held[mode]
                narrow[rows, :] = total
        mixed_ref[:, lanes] = narrow[...]
    gated = query_ref[...].astype(F32) * mixed_ref[...]
    gated_ref[...] = gated.astype(BF16)
    turned_ref[...] = gated.T.astype(BF16)


def stack_arrived(*refs):
    stack_blocks(refs[:5], refs[5])


def weight_part(position_ref, turned_ref, own_ref, other_ref, out_ref, token_ref, results, semaphores):
    place = position_ref[0]
    rank = position_ref[1]
    copies = []
    for ref, flip in ((own_ref, 0), (other_ref, 1)):
        for index, mask in enumerate(CHIP_MASKS):
            slot = mask | flip
            target = place ^ slot
            results[slot] = jnp.dot(
                turned_ref[...], ref[index], preferred_element_type=F32
            ).astype(BF16)
            copy = pltpu.make_async_copy(
                results.at[slot],
                out_ref.at[target & 7, lax.shift_right_logical(target ^ rank, 3)],
                semaphores.at[slot],
            )
            copy.start()
            copies.append(copy)
    token_ref[...] = jnp.zeros(token_ref.shape, F32)
    for copy in copies:
        copy.wait()


def project_rows(position_ref, query_ref, mixed_ref, gated_ref, out_weight_ref, own_ref, other_ref, query_grad_ref, drive_ref, sent_ref, mine_ref):
    place = position_ref[0]
    block = own_ref.shape[2]
    total = jnp.zeros(query_ref.shape, F32)
    for ref, flip, part_ref in ((other_ref, 1, sent_ref), (own_ref, 0, mine_ref)):
        for index, mask in enumerate(CHIP_MASKS):
            first = pl.multiple_of((place ^ (mask | flip)) * block, block)
            columns = out_weight_ref[:, pl.ds(first, block)]
            total = total + lax.dot_general(
                ref[index], columns, (((1,), (1,)), ((), ())), preferred_element_type=F32
            )
            part_ref[index] = jnp.dot(
                gated_ref[...], columns, preferred_element_type=F32
            ).astype(BF16)
    query_grad_ref[...] = (total * mixed_ref[...]).astype(BF16)
    drive_ref[...] = total * query_ref[...].astype(F32)


def backward_local(drive_ref, key_ref, value_ref, rate_ref, weight_ref, gain_ref, skip_ref, entering_ref, local_ref, sums_ref, product, carried):
    product[...] = key_ref[...].astype(F32) * value_ref[...].astype(F32)
    rates = rate_ref[...]
    weights = weight_ref[...]
    pole = jnp.exp(-rates)
    leap = jnp.exp(-float(SUB) * rates)
    state = jnp.zeros_like(rates)
    for block in reversed(range(SUB)):
        carried[pl.ds(block * SUB, SUB), :] = state
        inner = jnp.broadcast_to(drive_ref[pl.ds(block * SUB + SUB - 1, 1), :], rates.shape)
        for step in reversed(range(SUB - 1)):
            inner = pole * inner + drive_ref[pl.ds(block * SUB + step, 1), :]
        state = leap * state + inner
    sums_ref[pl.ds(0, SUB), :] = state
    sums_ref[pl.ds(SUB, SUB), :] = pole * entering_ref[...] * state
    sums_ref[pl.ds(2 * SUB, HALF), :] = jnp.zeros((HALF, LANES), F32)
    for half in range(2):
        drives = [strided(drive_ref, step, half) for step in range(SUB)]
        signal = [strided(product, step, half) for step in range(SUB)]
        totals = [skip_ref[...] * drive for drive in drives]
        direct = drives[0] * signal[0]
        for step in range(1, SUB):
            direct = direct + drives[step] * signal[step]
        sums_ref[pl.ds(2 * SUB, 1), :] += jnp.sum(direct, axis=0, keepdims=True)
        for mode in range(SUB):
            running = strided(carried, mode, half)
            gathered = jnp.zeros_like(running)
            for step in reversed(range(SUB)):
                running = pole[mode : mode + 1, :] * running + drives[step]
                totals[step] = totals[step] + weights[mode : mode + 1, :] * running
                gathered = gathered + signal[step] * running
            sums_ref[pl.ds(SUB + mode, 1), :] += jnp.sum(gathered, axis=0, keepdims=True)
        for step in range(SUB):
            local_ref[pl.ds(step + half * HALF * SUB, HALF, stride=SUB), :] = totals[step]
    sums_ref[pl.ds(SUB, SUB), :] *= gain_ref[...]


def backward_mix(position_ref, local_ref, key_ref, value_ref, rate_ref, weight_ref, inside_ref, whole_ref, first_ref, second_ref, third_ref, key_grad_ref, value_grad_ref, residue_ref, skip_sum_ref, scaled, grads):
    rates = rate_ref[...]
    tokens = local_ref.shape[0]
    across = [ref[pl.ds(0, SUB), :] for ref in (first_ref, second_ref, third_ref)]
    later = joined(True, tokens, position_ref, rates, inside_ref[...], across)
    pole = jnp.exp(-rates)
    power = weight_ref[...]
    for step in reversed(range(SUB)):
        power = power * pole
        scaled[pl.ds(step * SUB, SUB), :] = power
    for half in range(2):
        held = [
            block_decay(rates, mode, half, True) * later[mode : mode + 1, :] for mode in range(SUB)
        ]
        for step in range(SUB):
            total = strided(local_ref, step, half)
            for mode in range(SUB):
                total = total + scaled[pl.ds(step * SUB + mode, 1), :] * held[mode]
            grads[pl.ds(step + half * HALF * SUB, HALF, stride=SUB), :] = total
    product_grad = grads[...]
    key_grad_ref[...] = (product_grad * value_ref[...].astype(F32)).astype(BF16)
    value_grad_ref[...] = (product_grad * key_ref[...].astype(F32)).astype(BF16)
    for first, count, ref in ((SUB, SUB, residue_ref), (2 * SUB, 1, skip_sum_ref)):
        part = pl.ds(first, count)
        ref[...] = (whole_ref[part, :] + first_ref[part, :]) + (
            second_ref[part, :] + third_ref[part, :]
        )


def widened(ref, *place):
    return ref[place].astype(F32) if place else ref[...].astype(F32)


def merge_cores(mine_ref, other_ref, even_ref, odd_ref, rest_ref):
    for index, mask in enumerate(CHIP_MASKS):
        total = (widened(mine_ref, index) + widened(other_ref, index)).astype(BF16)
        if mask == 8:
            even_ref[...] = total
        elif mask == 10:
            odd_ref[...] = total
        else:
            rest_ref[index if mask < 8 else index - 2] = total


def merge_far(rest_ref, even_ref, odd_ref, first_ref, third_ref):
    first_ref[0] = rest_ref[2]
    first_ref[1] = (widened(rest_ref, 3) + widened(odd_ref)).astype(BF16)
    third_ref[0] = (widened(rest_ref, 4) + widened(even_ref)).astype(BF16)
    third_ref[1] = rest_ref[5]


def backward_near(tokens, position_ref, rate_ref, *rest):
    values = [ref[...] for ref in rest[:4]]
    near_sums(True, tokens, position_ref, rate_ref[...], values, rest[4], rest[5])


def merge_near(rest_ref, first_ref, third_ref, kept_ref, sent_ref):
    for index, ref in enumerate((kept_ref, sent_ref)):
        total = widened(rest_ref, index) + widened(first_ref, index) + widened(third_ref, index)
        ref[...] = total.astype(ref.dtype)


def merge_last(kept_ref, arrived_ref, out_ref):
    out_ref[...] = (kept_ref[...] + widened(arrived_ref)).astype(BF16)


VMEM = pl.BlockSpec(memory_space=pltpu.VMEM)
SMEM = pl.BlockSpec(memory_space=pltpu.SMEM)
ANY = pl.BlockSpec(memory_space=pl.ANY)


def tile_of(rows):
    return pl.BlockSpec((rows, LANES), lambda tile: (0, tile))


def shape_of(rows, columns, kind=F32):
    return jax.ShapeDtypeStruct((rows, columns), kind)


def ordered_call(body, ordered, in_specs, *operands, **options):
    count = len(ordered)

    def skipping(*refs):
        body(*refs[count:])

    return pl.pallas_call(skipping, in_specs=[ANY] * count + in_specs, **options)(
        *ordered, *operands
    )


def granted(mebibytes):
    return pltpu.CompilerParams(vmem_limit_bytes=mebibytes * 1024 * 1024)


def kind_of(*shape, dtype=BF16):
    return jax.ShapeDtypeStruct(shape, dtype)


def local_call(body, out_shape, *operands, ordered=(), scalars=0, scratch=(), limit=11):
    plain = body.func if isinstance(body, functools.partial) else body
    return ordered_call(
        body,
        ordered,
        [SMEM] * scalars
        + [VMEM] * (len(operands) - scalars),
        *operands,
        out_specs=[VMEM] * len(out_shape),
        out_shape=out_shape,
        scratch_shapes=scratch,
        compiler_params=granted(limit),
        name=plain.__name__,
    )


def on_device(query_rows, key_rows, value_rows, residues, decays, skip_gain, out_weight, cotangent):
    tokens, width = query_rows.shape
    modes = residues.shape[0]
    ctx_count = lax.axis_size("ctx")
    chan_count = lax.axis_size("chan")
    positions = jnp.stack([lax.axis_index("chan"), lax.axis_index("ctx")]).astype(jnp.int32)
    skip_row = skip_gain.reshape(1, width)
    tiles = width // LANES
    rows = tile_of(tokens)
    few = tile_of(modes)
    one = tile_of(1)
    tall = 2 * modes + HALF
    sums = tile_of(tall)
    block_scratch = pltpu.VMEM((tokens, LANES), F32)
    columns = cotangent.shape[1]
    block = kind_of(tokens, columns)
    pair_block = kind_of(2, tokens, columns)
    eight = kind_of(8, tokens, columns)
    square = shape_of(tokens, width)
    state_shape = shape_of(modes, width)
    tall_shape = shape_of(tall, width)

    arrived = traded(cotangent, "chan", 2)
    state, local, rates, gains, weights = pl.pallas_call(
        functools.partial(forward_local, tokens * ctx_count),
        grid=(tiles,),
        in_specs=[rows, rows, few, few, one],
        out_specs=[tile_of(2 * modes), rows, few, few, few],
        out_shape=[shape_of(2 * modes, width), square, state_shape, state_shape, state_shape],
        scratch_shapes=[block_scratch] * 3,
        name="forward_local",
    )(key_rows, value_rows, decays, residues, skip_row)
    near = [state] + [traded(state, "ctx", mask) for mask in (1, 2, 3)]
    inside, whole, pair = local_call(
        functools.partial(forward_near, tokens),
        [state_shape, state_shape, pair_block],
        positions,
        *near,
        cotangent,
        arrived,
        scalars=1,
    )

    first, third = traded(pair, "chan", 4), traded(pair, "chan", 12)
    across = [traded(whole, "ctx", 4 * mask) for mask in (1, 2, 3)]
    far = local_call(open_far, [block, block], first, third, ordered=across)
    mixed, gated, gated_turned, entering = local_call(
        forward_mix,
        [square, kind_of(tokens, width), kind_of(width, tokens), state_shape],
        positions,
        local,
        query_rows,
        rates,
        weights,
        inside,
        *across,
        ordered=far[:1],
        scalars=1,
        scratch=[block_scratch] * 2,
    )

    even, odd = traded(far[0], "chan", 12), traded(far[1], "chan", 4)
    own = local_call(stack_arrived, [eight], pair, first, third, even, odd)[0]

    sibling = traded(own, "chan", 1)
    weight_share, token = pl.pallas_call(
        weight_part,
        in_specs=[SMEM] + [VMEM] * 3,
        out_specs=[pl.BlockSpec(memory_space=pltpu.HBM), VMEM],
        out_shape=[pltpu.HBM((8, 2, width, columns), BF16), shape_of(HALF, LANES)],
        scratch_shapes=[
            pltpu.VMEM((ctx_count, width, columns), BF16),
            pltpu.SemaphoreType.DMA((ctx_count,)),
        ],
        compiler_params=granted(11),
        name="weight_part",
    )(positions, gated_turned, own, sibling)
    weight_grad = lax.psum_scatter(
        weight_share,
        "ctx",
        scatter_dimension=0,
        axis_index_groups=[list(range(8)), list(range(8, 16))],
        tiled=False,
    )
    query_grad, drive, other, mine = local_call(
        project_rows,
        [kind_of(tokens, width), square, eight, eight],
        positions,
        query_rows,
        mixed,
        gated,
        out_weight,
        own,
        sibling,
        ordered=[token],
        scalars=1,
        limit=14,
    )
    back_local, back_state = pl.pallas_call(
        backward_local,
        grid=(tiles,),
        in_specs=[rows, rows, rows, few, few, few, one, few],
        out_specs=[rows, sums],
        out_shape=[square, tall_shape],
        scratch_shapes=[block_scratch] * 2,
        name="backward_local",
    )(drive, key_rows, value_rows, rates, weights, gains, skip_row, entering)
    even, odd, rest = local_call(
        merge_cores,
        [block, block, kind_of(6, tokens, columns)],
        mine,
        traded(other, "chan", 1),
        ordered=[back_state],
    )

    near = [back_state] + [traded(back_state, "ctx", mask) for mask in (1, 2, 3)]
    inside, whole = local_call(
        functools.partial(backward_near, tokens),
        [state_shape, tall_shape],
        positions,
        rates,
        *near,
        scalars=1,
    )
    first, third = local_call(
        merge_far,
        [pair_block, pair_block],
        rest,
        traded(even, "chan", 4),
        traded(odd, "chan", 12),
        ordered=[whole],
    )

    across = [traded(whole, "ctx", 4 * mask) for mask in (1, 2, 3)]
    kept, sent = local_call(
        merge_near,
        [shape_of(tokens, columns), block],
        rest,
        traded(first, "chan", 4),
        traded(third, "chan", 12),
        ordered=across,
    )

    layer_out = local_call(
        merge_last, [kind_of(tokens, columns)], kept, traded(sent, "chan", 2)
    )[0]
    key_grad, value_grad, residue_grad, skip_sum = pl.pallas_call(
        backward_mix,
        grid=(tiles,),
        in_specs=[SMEM, rows, rows, rows, few, few, few] + [sums] * 4,
        out_specs=[rows, rows, few, one],
        out_shape=[
            kind_of(tokens, width),
            kind_of(tokens, width),
            state_shape,
            shape_of(1, width),
        ],
        scratch_shapes=[block_scratch] * 2,
        name="backward_mix",
    )(positions, back_local, key_rows, value_rows, rates, weights, inside, whole, *across)
    arrived = traded(weight_grad[1], "ctx", 8)
    weight_grad = weight_grad[0].astype(F32) + arrived.astype(F32)
    return (
        layer_out,
        query_grad,
        key_grad,
        value_grad,
        residue_grad,
        skip_sum.reshape(width),
        weight_grad,
    )


def solution(mesh):
    placed = (
        P("ctx", "chan"),
        P("ctx", "chan"),
        P("ctx", "chan"),
        P(None, "chan"),
        P(None, "chan"),
        P("chan"),
        P("chan", None),
        P("ctx", "chan"),
    )
    return jax.shard_map(
        on_device,
        mesh=mesh,
        in_specs=placed,
        out_specs=(
            P("ctx", "chan"),
            P("ctx", "chan"),
            P("ctx", "chan"),
            P("ctx", "chan"),
            P(None, "chan"),
            P("chan"),
            P("chan", "ctx"),
        ),
        check_vma=False,
    )
```

```python
import functools

import jax
import jax.numpy as jnp
from jax import lax
from jax.experimental import pallas as pl
from jax.experimental.pallas import tpu as pltpu
from jax.sharding import PartitionSpec as P

F32 = jnp.float32
BF16 = jnp.bfloat16
LANES = 128
SUB = 16
HALF = 8
CHIP_MASKS = tuple(range(0, 16, 2))


def traded(value, axis, mask):
    pairs = [(source, source ^ mask) for source in range(lax.axis_size(axis))]
    return lax.ppermute(value, axis, pairs)


def strided(ref, offset, half):
    return ref[pl.ds(offset + half * HALF * SUB, HALF, stride=SUB), :]


def shortfall(value):
    series = jnp.ones_like(value)
    for order in range(10, 1, -1):
        series = 1.0 - value * (1.0 / order) * series
    return jnp.where(value < 0.5, value * series, 1.0 - jnp.exp(-value))


def forward_state(length, key_ref, value_ref, decay_ref, residue_ref, state_ref, rate_ref, gain_ref, weight_ref, product):
    product[...] = key_ref[...].astype(F32) * value_ref[...].astype(F32)
    rates = decay_ref[...] * (1.0 / length)
    gains = jnp.sqrt(shortfall(2.0 * rates) * (1.0 / rates.shape[0]))
    pole = jnp.exp(-rates)
    leap = jnp.exp(-float(SUB) * rates)
    state = jnp.zeros_like(rates)
    for block in range(SUB):
        inner = jnp.broadcast_to(product[pl.ds(block * SUB, 1), :], rates.shape)
        for step in range(1, SUB):
            inner = pole * inner + product[pl.ds(block * SUB + step, 1), :]
        state = leap * state + inner
    state_ref[pl.ds(0, SUB), :] = state
    state_ref[pl.ds(SUB, SUB), :] = rates
    rate_ref[...] = rates
    gain_ref[...] = gains
    weight_ref[...] = residue_ref[...] * gains


def forward_local(key_ref, value_ref, rate_ref, weight_ref, skip_ref, mixed_ref, token_ref, product, carried, scaled):
    product[...] = key_ref[...].astype(F32) * value_ref[...].astype(F32)
    rates = rate_ref[...]
    weights = weight_ref[...]
    pole = jnp.exp(-rates)
    leap = jnp.exp(-float(SUB) * rates)
    state = jnp.zeros_like(rates)
    for block in range(SUB):
        carried[pl.ds(block * SUB, SUB), :] = state
        inner = jnp.broadcast_to(product[pl.ds(block * SUB, 1), :], rates.shape)
        for step in range(1, SUB):
            inner = pole * inner + product[pl.ds(block * SUB + step, 1), :]
        state = leap * state + inner
    token_ref[...] = jnp.zeros(token_ref.shape, F32)
    taps = []
    power = weights
    for step in range(SUB):
        taps.append(jnp.sum(power, axis=0, keepdims=True))
        power = power * pole
        scaled[pl.ds(step * SUB, SUB), :] = power
    taps[0] = taps[0] + skip_ref[...]
    for half in range(2):
        held = [strided(carried, mode, half) for mode in range(SUB)]
        signal = [strided(product, step, half) for step in range(SUB)]
        for step in range(SUB):
            total = taps[0] * signal[step]
            for lag in range(1, step + 1):
                total = total + taps[lag] * signal[step - lag]
            for mode in range(SUB):
                total = total + scaled[pl.ds(step * SUB + mode, 1), :] * held[mode]
            mixed_ref[pl.ds(step + half * HALF * SUB, HALF, stride=SUB), :] = total


def block_decay(rates, mode, half, backward):
    place = lax.broadcasted_iota(jnp.int32, (HALF, LANES), 0).astype(F32) + float(half * HALF)
    distance = float(SUB - 1) - place if backward else place
    return jnp.exp(-float(SUB) * distance * rates[mode : mode + 1, :])


def falling(rates, distance):
    reach = jnp.maximum(distance, 0).astype(F32)
    present = jnp.where(distance >= 0, 1.0, 0.0).astype(F32)
    return jnp.exp(-reach * rates) * present


def near_sums(backward, tokens, position_ref, rates, values, inside_ref, whole_ref):
    modes = rates.shape[0]
    low = position_ref[1] & 3
    inside = jnp.zeros_like(rates)
    whole = jnp.zeros_like(rates)
    for mask in range(4):
        spot = low ^ mask
        state = values[mask][:modes]
        gap = spot - low - 1 if backward else low - 1 - spot
        far = spot if backward else 3 - spot
        inside = inside + falling(rates, tokens * gap) * state
        whole = whole + falling(rates, tokens * far) * state
    inside_ref[...] = inside
    whole_ref[pl.ds(0, modes), :] = whole
    if backward:
        sums = [value[modes:] for value in values]
        whole_ref[pl.ds(modes, sums[0].shape[0]), :] = (sums[0] + sums[1]) + (sums[2] + sums[3])


def forward_near(tokens, position_ref, *rest):
    own_ref, arrived_ref, inside_ref, whole_ref, pair_ref = rest[4:]
    values = [ref[...] for ref in rest[:4]]
    rates = values[0][values[0].shape[0] // 2 :]
    near_sums(False, tokens, position_ref, rates, values, inside_ref, whole_ref)
    pair_ref[0] = own_ref[...]
    pair_ref[1] = arrived_ref[...]


def open_far(first_ref, third_ref, even_ref, odd_ref):
    even_ref[...] = first_ref[0]
    odd_ref[...] = third_ref[1]


def stack_blocks(refs, out_ref):
    pair, first, third, even, odd = refs
    for index, block in enumerate((pair.at[0], pair.at[1], first.at[0], first.at[1])):
        out_ref[index] = block[...]
    for index, block in enumerate((even, odd, third.at[0], third.at[1])):
        out_ref[4 + index] = block[...]


def joined(backward, tokens, position_ref, rates, inside, across):
    low = position_ref[1] & 3
    high = lax.shift_right_logical(position_ref[1], 2)
    total = jnp.zeros_like(rates)
    for mask in range(1, 4):
        spot = high ^ mask
        gap = spot - high - 1 if backward else high - 1 - spot
        total = total + falling(rates, 4 * tokens * gap) * across[mask - 1]
    span = 3 - low if backward else low
    return inside + falling(rates, tokens * span) * total


def forward_mix(position_ref, local_ref, query_ref, rate_ref, weight_ref, inside_ref, first_ref, second_ref, third_ref, mixed_ref, gated_ref, turned_ref, entering_ref, scaled, narrow):
    tokens = local_ref.shape[0]
    for tile in range(2):
        lanes = pl.ds(tile * LANES, LANES)
        narrow[...] = local_ref[:, lanes]
        rates = rate_ref[:, lanes]
        weights = weight_ref[:, lanes]
        across = [ref[:, lanes] for ref in (first_ref, second_ref, third_ref)]
        entering = joined(False, tokens, position_ref, rates, inside_ref[:, lanes], across)
        entering_ref[:, lanes] = entering
        pole = jnp.exp(-rates)
        power = weights
        for step in range(SUB):
            power = power * pole
            scaled[pl.ds(step * SUB, SUB), :] = power
        for half in range(2):
            held = [
                block_decay(rates, mode, half, False) * entering[mode : mode + 1, :]
                for mode in range(SUB)
            ]
            for step in range(SUB):
                rows = pl.ds(step + half * HALF * SUB, HALF, stride=SUB)
                total = narrow[rows, :]
                for mode in range(SUB):
                    total = total + scaled[pl.ds(step * SUB + mode, 1), :] * held[mode]
                narrow[rows, :] = total
        mixed_ref[:, lanes] = narrow[...]
    gated = query_ref[...].astype(F32) * mixed_ref[...]
    gated_ref[...] = gated.astype(BF16)
    turned_ref[...] = gated.T.astype(BF16)


def stack_arrived(*refs):
    stack_blocks(refs[:5], refs[5])


def weight_part(position_ref, turned_ref, own_ref, other_ref, out_ref, token_ref, results, semaphores):
    place = position_ref[0]
    rank = position_ref[1]
    copies = []
    for ref, flip in ((own_ref, 0), (other_ref, 1)):
        for index, mask in enumerate(CHIP_MASKS):
            slot = mask | flip
            target = place ^ slot
            results[slot] = jnp.dot(
                turned_ref[...], ref[index], preferred_element_type=F32
            ).astype(BF16)
            copy = pltpu.make_async_copy(
                results.at[slot],
                out_ref.at[target & 7, lax.shift_right_logical(target ^ rank, 3)],
                semaphores.at[slot],
            )
            copy.start()
            copies.append(copy)
    token_ref[...] = jnp.zeros(token_ref.shape, F32)
    for copy in copies:
        copy.wait()


def project_rows(position_ref, query_ref, mixed_ref, gated_ref, out_weight_ref, own_ref, other_ref, query_grad_ref, drive_ref, sent_ref, mine_ref):
    place = position_ref[0]
    block = own_ref.shape[2]
    total = jnp.zeros(query_ref.shape, F32)
    for ref, flip, part_ref in ((other_ref, 1, sent_ref), (own_ref, 0, mine_ref)):
        for index, mask in enumerate(CHIP_MASKS):
            first = pl.multiple_of((place ^ (mask | flip)) * block, block)
            columns = out_weight_ref[:, pl.ds(first, block)]
            total = total + lax.dot_general(
                ref[index], columns, (((1,), (1,)), ((), ())), preferred_element_type=F32
            )
            part_ref[index] = jnp.dot(
                gated_ref[...], columns, preferred_element_type=F32
            ).astype(BF16)
    query_grad_ref[...] = (total * mixed_ref[...]).astype(BF16)
    drive_ref[...] = total * query_ref[...].astype(F32)


def backward_local(drive_ref, key_ref, value_ref, rate_ref, weight_ref, gain_ref, skip_ref, entering_ref, local_ref, sums_ref, product, carried):
    product[...] = key_ref[...].astype(F32) * value_ref[...].astype(F32)
    rates = rate_ref[...]
    weights = weight_ref[...]
    pole = jnp.exp(-rates)
    leap = jnp.exp(-float(SUB) * rates)
    state = jnp.zeros_like(rates)
    for block in reversed(range(SUB)):
        carried[pl.ds(block * SUB, SUB), :] = state
        inner = jnp.broadcast_to(drive_ref[pl.ds(block * SUB + SUB - 1, 1), :], rates.shape)
        for step in reversed(range(SUB - 1)):
            inner = pole * inner + drive_ref[pl.ds(block * SUB + step, 1), :]
        state = leap * state + inner
    sums_ref[pl.ds(0, SUB), :] = state
    sums_ref[pl.ds(SUB, SUB), :] = pole * entering_ref[...] * state
    sums_ref[pl.ds(2 * SUB, HALF), :] = jnp.zeros((HALF, LANES), F32)
    for half in range(2):
        drives = [strided(drive_ref, step, half) for step in range(SUB)]
        signal = [strided(product, step, half) for step in range(SUB)]
        totals = [skip_ref[...] * drive for drive in drives]
        direct = drives[0] * signal[0]
        for step in range(1, SUB):
            direct = direct + drives[step] * signal[step]
        sums_ref[pl.ds(2 * SUB, 1), :] += jnp.sum(direct, axis=0, keepdims=True)
        for mode in range(SUB):
            running = strided(carried, mode, half)
            gathered = jnp.zeros_like(running)
            for step in reversed(range(SUB)):
                running = pole[mode : mode + 1, :] * running + drives[step]
                totals[step] = totals[step] + weights[mode : mode + 1, :] * running
                gathered = gathered + signal[step] * running
            sums_ref[pl.ds(SUB + mode, 1), :] += jnp.sum(gathered, axis=0, keepdims=True)
        for step in range(SUB):
            local_ref[pl.ds(step + half * HALF * SUB, HALF, stride=SUB), :] = totals[step]
    sums_ref[pl.ds(SUB, SUB), :] *= gain_ref[...]


def backward_mix(position_ref, local_ref, key_ref, value_ref, rate_ref, weight_ref, inside_ref, whole_ref, first_ref, second_ref, third_ref, key_grad_ref, value_grad_ref, residue_ref, skip_sum_ref, scaled, grads):
    rates = rate_ref[...]
    tokens = local_ref.shape[0]
    across = [ref[pl.ds(0, SUB), :] for ref in (first_ref, second_ref, third_ref)]
    later = joined(True, tokens, position_ref, rates, inside_ref[...], across)
    pole = jnp.exp(-rates)
    power = weight_ref[...]
    for step in reversed(range(SUB)):
        power = power * pole
        scaled[pl.ds(step * SUB, SUB), :] = power
    for half in range(2):
        held = [
            block_decay(rates, mode, half, True) * later[mode : mode + 1, :] for mode in range(SUB)
        ]
        for step in range(SUB):
            total = strided(local_ref, step, half)
            for mode in range(SUB):
                total = total + scaled[pl.ds(step * SUB + mode, 1), :] * held[mode]
            grads[pl.ds(step + half * HALF * SUB, HALF, stride=SUB), :] = total
    product_grad = grads[...]
    key_grad_ref[...] = (product_grad * value_ref[...].astype(F32)).astype(BF16)
    value_grad_ref[...] = (product_grad * key_ref[...].astype(F32)).astype(BF16)
    for first, count, ref in ((SUB, SUB, residue_ref), (2 * SUB, 1, skip_sum_ref)):
        part = pl.ds(first, count)
        ref[...] = (whole_ref[part, :] + first_ref[part, :]) + (
            second_ref[part, :] + third_ref[part, :]
        )


def widened(ref, *place):
    return ref[place].astype(F32) if place else ref[...].astype(F32)


def merge_cores(mine_ref, other_ref, even_ref, odd_ref, rest_ref):
    for index, mask in enumerate(CHIP_MASKS):
        total = (widened(mine_ref, index) + widened(other_ref, index)).astype(BF16)
        if mask == 8:
            even_ref[...] = total
        elif mask == 10:
            odd_ref[...] = total
        else:
            rest_ref[index if mask < 8 else index - 2] = total


def merge_far(rest_ref, even_ref, odd_ref, first_ref, third_ref):
    first_ref[0] = rest_ref[2]
    first_ref[1] = (widened(rest_ref, 3) + widened(odd_ref)).astype(BF16)
    third_ref[0] = (widened(rest_ref, 4) + widened(even_ref)).astype(BF16)
    third_ref[1] = rest_ref[5]


def backward_near(tokens, position_ref, rate_ref, *rest):
    values = [ref[...] for ref in rest[:4]]
    near_sums(True, tokens, position_ref, rate_ref[...], values, rest[4], rest[5])


def merge_near(rest_ref, first_ref, third_ref, kept_ref, sent_ref):
    for index, ref in enumerate((kept_ref, sent_ref)):
        total = widened(rest_ref, index) + widened(first_ref, index) + widened(third_ref, index)
        ref[...] = total.astype(ref.dtype)


def merge_last(kept_ref, arrived_ref, out_ref):
    out_ref[...] = (kept_ref[...] + widened(arrived_ref)).astype(BF16)


VMEM = pl.BlockSpec(memory_space=pltpu.VMEM)
SMEM = pl.BlockSpec(memory_space=pltpu.SMEM)
ANY = pl.BlockSpec(memory_space=pl.ANY)


def tile_of(rows):
    return pl.BlockSpec((rows, LANES), lambda tile: (0, tile))


def shape_of(rows, columns, kind=F32):
    return jax.ShapeDtypeStruct((rows, columns), kind)


def ordered_call(body, ordered, in_specs, *operands, **options):
    count = len(ordered)

    def skipping(*refs):
        body(*refs[count:])

    return pl.pallas_call(skipping, in_specs=[ANY] * count + in_specs, **options)(
        *ordered, *operands
    )


def granted(mebibytes):
    return pltpu.CompilerParams(vmem_limit_bytes=mebibytes * 1024 * 1024)


def kind_of(*shape, dtype=BF16):
    return jax.ShapeDtypeStruct(shape, dtype)


def local_call(body, out_shape, *operands, ordered=(), scalars=0, scratch=(), limit=11):
    plain = body.func if isinstance(body, functools.partial) else body
    return ordered_call(
        body,
        ordered,
        [SMEM] * scalars
        + [VMEM] * (len(operands) - scalars),
        *operands,
        out_specs=[VMEM] * len(out_shape),
        out_shape=out_shape,
        scratch_shapes=scratch,
        compiler_params=granted(limit),
        name=plain.__name__,
    )


def on_device(query_rows, key_rows, value_rows, residues, decays, skip_gain, out_weight, cotangent):
    tokens, width = query_rows.shape
    modes = residues.shape[0]
    ctx_count = lax.axis_size("ctx")
    chan_count = lax.axis_size("chan")
    positions = jnp.stack([lax.axis_index("chan"), lax.axis_index("ctx")]).astype(jnp.int32)
    skip_row = skip_gain.reshape(1, width)
    tiles = width // LANES
    rows = tile_of(tokens)
    few = tile_of(modes)
    one = tile_of(1)
    tall = 2 * modes + HALF
    sums = tile_of(tall)
    block_scratch = pltpu.VMEM((tokens, LANES), F32)
    columns = cotangent.shape[1]
    block = kind_of(tokens, columns)
    pair_block = kind_of(2, tokens, columns)
    eight = kind_of(8, tokens, columns)
    square = shape_of(tokens, width)
    state_shape = shape_of(modes, width)
    tall_shape = shape_of(tall, width)

    arrived = traded(cotangent, "chan", 2)
    state, rates, gains, weights = pl.pallas_call(
        functools.partial(forward_state, tokens * ctx_count),
        grid=(tiles,),
        in_specs=[rows, rows, few, few],
        out_specs=[tile_of(2 * modes), few, few, few],
        out_shape=[shape_of(2 * modes, width), state_shape, state_shape, state_shape],
        scratch_shapes=[block_scratch],
        name="forward_state",
    )(key_rows, value_rows, decays, residues)
    local, local_token = pl.pallas_call(
        forward_local,
        grid=(tiles,),
        in_specs=[rows, rows, few, few, one],
        out_specs=[rows, tile_of(HALF)],
        out_shape=[square, shape_of(HALF, width)],
        scratch_shapes=[block_scratch] * 3,
        name="forward_local",
    )(key_rows, value_rows, rates, weights, skip_row)
    near = [state] + [traded(state, "ctx", mask) for mask in (1, 2, 3)]
    inside, whole, pair = local_call(
        functools.partial(forward_near, tokens),
        [state_shape, state_shape, pair_block],
        positions,
        *near,
        cotangent,
        arrived,
        ordered=[local_token],
        scalars=1,
    )

    first, third = traded(pair, "chan", 4), traded(pair, "chan", 12)
    across = [traded(whole, "ctx", 4 * mask) for mask in (1, 2, 3)]
    far = local_call(open_far, [block, block], first, third, ordered=across)
    mixed, gated, gated_turned, entering = local_call(
        forward_mix,
        [square, kind_of(tokens, width), kind_of(width, tokens), state_shape],
        positions,
        local,
        query_rows,
        rates,
        weights,
        inside,
        *across,
        ordered=far[:1],
        scalars=1,
        scratch=[block_scratch] * 2,
    )

    even, odd = traded(far[0], "chan", 12), traded(far[1], "chan", 4)
    own = local_call(stack_arrived, [eight], pair, first, third, even, odd)[0]

    sibling = traded(own, "chan", 1)
    weight_share, token = pl.pallas_call(
        weight_part,
        in_specs=[SMEM] + [VMEM] * 3,
        out_specs=[pl.BlockSpec(memory_space=pltpu.HBM), VMEM],
        out_shape=[pltpu.HBM((8, 2, width, columns), BF16), shape_of(HALF, LANES)],
        scratch_shapes=[
            pltpu.VMEM((ctx_count, width, columns), BF16),
            pltpu.SemaphoreType.DMA((ctx_count,)),
        ],
        compiler_params=granted(11),
        name="weight_part",
    )(positions, gated_turned, own, sibling)
    weight_grad = lax.psum_scatter(
        weight_share,
        "ctx",
        scatter_dimension=0,
        axis_index_groups=[list(range(8)), list(range(8, 16))],
        tiled=False,
    )
    query_grad, drive, other, mine = local_call(
        project_rows,
        [kind_of(tokens, width), square, eight, eight],
        positions,
        query_rows,
        mixed,
        gated,
        out_weight,
        own,
        sibling,
        ordered=[token],
        scalars=1,
        limit=14,
    )
    back_local, back_state = pl.pallas_call(
        backward_local,
        grid=(tiles,),
        in_specs=[rows, rows, rows, few, few, few, one, few],
        out_specs=[rows, sums],
        out_shape=[square, tall_shape],
        scratch_shapes=[block_scratch] * 2,
        name="backward_local",
    )(drive, key_rows, value_rows, rates, weights, gains, skip_row, entering)
    even, odd, rest = local_call(
        merge_cores,
        [block, block, kind_of(6, tokens, columns)],
        mine,
        traded(other, "chan", 1),
        ordered=[back_state],
    )

    near = [back_state] + [traded(back_state, "ctx", mask) for mask in (1, 2, 3)]
    inside, whole = local_call(
        functools.partial(backward_near, tokens),
        [state_shape, tall_shape],
        positions,
        rates,
        *near,
        scalars=1,
    )
    first, third = local_call(
        merge_far,
        [pair_block, pair_block],
        rest,
        traded(even, "chan", 4),
        traded(odd, "chan", 12),
        ordered=[whole],
    )

    across = [traded(whole, "ctx", 4 * mask) for mask in (1, 2, 3)]
    kept, sent = local_call(
        merge_near,
        [shape_of(tokens, columns), block],
        rest,
        traded(first, "chan", 4),
        traded(third, "chan", 12),
        ordered=across,
    )

    layer_out = local_call(
        merge_last, [kind_of(tokens, columns)], kept, traded(sent, "chan", 2)
    )[0]
    key_grad, value_grad, residue_grad, skip_sum = pl.pallas_call(
        backward_mix,
        grid=(tiles,),
        in_specs=[SMEM, rows, rows, rows, few, few, few] + [sums] * 4,
        out_specs=[rows, rows, few, one],
        out_shape=[
            kind_of(tokens, width),
            kind_of(tokens, width),
            state_shape,
            shape_of(1, width),
        ],
        scratch_shapes=[block_scratch] * 2,
        name="backward_mix",
    )(positions, back_local, key_rows, value_rows, rates, weights, inside, whole, *across)
    arrived = traded(weight_grad[1], "ctx", 8)
    weight_grad = weight_grad[0].astype(F32) + arrived.astype(F32)
    return (
        layer_out,
        query_grad,
        key_grad,
        value_grad,
        residue_grad,
        skip_sum.reshape(width),
        weight_grad,
    )


def solution(mesh):
    placed = (
        P("ctx", "chan"),
        P("ctx", "chan"),
        P("ctx", "chan"),
        P(None, "chan"),
        P(None, "chan"),
        P("chan"),
        P("chan", None),
        P("ctx", "chan"),
    )
    return jax.shard_map(
        on_device,
        mesh=mesh,
        in_specs=placed,
        out_specs=(
            P("ctx", "chan"),
            P("ctx", "chan"),
            P("ctx", "chan"),
            P("ctx", "chan"),
            P(None, "chan"),
            P("chan"),
            P("chan", "ctx"),
        ),
        check_vma=False,
    )
```
